128 devices in a mesh: dp: 8 (over z, x_hi), ctx: 16 (over x_lo, y, core).
Axes of the slice: x: 4 (x_hi: 2, x_lo: 2; x = x_hi * 2 + x_lo), y: 4, z: 4, core: 2. Of those that a mesh axis runs over, the one named last changes fastest.
Arguments:
- hidden: bfloat16 [65536, 4096], P(('dp', 'ctx')), parts along dimension 0, may hold values from -24 to 24
- dest: int32 [65536], P(('dp', 'ctx')), parts along dimension 0, may hold values from 0 to 8191, as said below
- doc_ids: int32 [65536], P('dp'), parts along dimension 0, may hold values from 0 to 63, never falling along the last dimension, each value on 1 to 1024 neighbouring positions
- w_query: bfloat16 [4096, 2048], P('ctx'), may hold values from -0.09375 to 0.09375
- key_weight: bfloat16 [4096, 512], P('ctx'), may hold values from -0.09375 to 0.09375
- value_weight: bfloat16 [4096, 512], P('ctx'), may hold values from -0.09375 to 0.09375
Outputs:
- attended: bfloat16 [65536, 2048], P(('dp', 'ctx')), parts along dimension 0
The draws below stay inside these ranges and needn't reach their ends.
There are 8 independent parts, one for each index of `dp`. The reference program is written for one: setup_inputs(seed, part) draws one part's arguments, and reference() takes and returns one part's arrays. A program takes and returns all parts, laid end to end along the dimension named above; an argument that names none is the same for every part. Nothing has to cross between parts.
Inputs may be any that keep to these rules, and one draw needn't show every extreme that they name: `dest`: A permutation. Each block of 512 loader rows sends at most 64 rows to one block of 512 context positions, exactly 64 to some.
All inputs are finite; a program needn't handle non-finite values.
Results may differ from the reference program's by a relative error of at most 0.024.
Values may be sent and summed in bfloat16 or wider, within the bound.
A program may use at most 128 MiB of HBM per device.

```python
import math
import jax
import jax.numpy as jnp
import numpy as np
from jax import lax

MODEL_WIDTH = 4096
QUERY_HEADS = 16
KEY_VALUE_HEADS = 4
HEAD_SIZE = 128
BLOCK_TOKENS = 512
SEQ = 8192
DOCS = 64
N_CTX = 16


def draw_hidden(key, part):
    values_drawn = jnp.clip(jax.random.normal(key, (SEQ, MODEL_WIDTH), jnp.float32), -4.0, 4.0)
    return values_drawn.astype(jnp.bfloat16)


def draw_dest(key, part):
    cycle_size = N_CTX
    rows_dev = BLOCK_TOKENS
    capacity = 2 * rows_dev // cycle_size
    shift_key = jax.random.fold_in(key, 11)
    source_key = jax.random.fold_in(key, 13)
    target_key = jax.random.fold_in(key, 17)
    shifts = jax.random.permutation(shift_key, cycle_size)
    piece_count = 3 * cycle_size // 4
    counts = jnp.where(jnp.arange(piece_count) < cycle_size // 4, capacity, capacity // 2)
    piece_ends = jnp.cumsum(counts)
    slots = jnp.arange(rows_dev, dtype=jnp.int32)
    piece_of = jnp.sum((slots[:, None] >= piece_ends[None, :]).astype(jnp.int32), axis=1)
    shift_of = shifts[piece_of]
    sigma = jax.vmap(lambda sub_key: jax.random.permutation(sub_key, rows_dev))(jax.random.split(source_key, cycle_size))
    tau_table = jax.vmap(lambda sub_key: jax.random.permutation(sub_key, rows_dev))(jax.random.split(target_key, cycle_size))
    sources = jnp.arange(cycle_size, dtype=jnp.int32)[:, None]
    owners = (sources + shift_of[None, :]) % cycle_size
    loader = sources * rows_dev + sigma
    target = owners * rows_dev + tau_table[owners, slots[None, :]]
    result = jnp.zeros((SEQ,), jnp.int32).at[loader.reshape(-1)].set(target.reshape(-1).astype(jnp.int32))
    return result


def levels(stream_key, dims, shards, low, high):
    def one(dim, parts):
        heights = jax.random.uniform(jax.random.fold_in(jax.random.fold_in(stream_key, 6), dim), (parts,), jnp.float32, low / len(shards), high / len(shards))
        return jnp.repeat(jnp.exp(heights), dims[dim] // parts).reshape((-1,) + (1,) * (len(dims) - dim - 1))

    level = one(*shards[0])
    for cut in shards[1:]:
        level = level * one(*cut)
    return level


def profile(amount, total, most, slope):
    weights = [(1 << 20) // math.isqrt(rank ** slope) + 1 for rank in range(2, amount + 1)]
    spare, given = total - most - (amount - 1), [1] * (amount - 1)
    while spare > 0:
        movable = [i for i in range(amount - 1) if given[i] < most]
        mass, left = sum([weights[i] for i in movable]), spare
        for i in movable:
            more = min(most - given[i], max(1, left * weights[i] // mass), spare)
            given[i] = given[i] + more
            spare = spare - more
    return np.array([most] + given)


def uneven_parts(rng, number_of, total, bound, slope):
    if number_of == 2:
        one = jax.random.randint(rng, (), max(1, total - bound), min(bound, total - 1) + 1)
        return jnp.stack([one, total - one])
    sizes = jnp.asarray(profile(number_of, total, bound, slope), jnp.int32)
    couples = (number_of - 1) // 2
    source_of, taker = sizes[1:1 + 2 * couples:2], sizes[2:2 + 2 * couples:2]
    slack = jnp.minimum(source_of - 1, bound - taker)
    shifted = jax.random.randint(jax.random.fold_in(rng, 1), (couples,), 0, 1 << 20) % (slack + 1)
    sizes = sizes.at[1:1 + 2 * couples:2].set(source_of - shifted).at[2:2 + 2 * couples:2].set(taker + shifted)
    return sizes[jax.random.permutation(jax.random.fold_in(rng, 2), number_of)]


def noise(key, extent, scale, most, cuts=(), kind=jnp.bfloat16):
    drawn = scale * jax.random.normal(key, extent, jnp.float32)
    if cuts:
        drawn = drawn * levels(key, extent, cuts, -0.22, 0.18)
    return jnp.clip(drawn, -most, most).astype(kind)


def setup_inputs(seed: int = 0, part: int = 0) -> dict:
    arg_keys = jax.random.split(jax.random.key(seed), 7)
    own_keys = jax.random.split(jax.random.fold_in(arg_keys[6], part), 7)
    return {
        "hidden": draw_hidden(jax.random.fold_in(jax.random.fold_in(arg_keys[6], part), 71), part),
        "dest": draw_dest(jax.random.fold_in(jax.random.fold_in(arg_keys[6], part), 71), part),
        "doc_ids": jnp.searchsorted(jnp.cumsum(uneven_parts(own_keys[2], DOCS, SEQ, 2 * BLOCK_TOKENS, 2)), jnp.arange(SEQ), side="right").astype(jnp.int32),
        "w_query": noise(arg_keys[3], (MODEL_WIDTH, QUERY_HEADS * HEAD_SIZE), MODEL_WIDTH ** -0.5, 0.09375, ((0, 16),)),
        "key_weight": noise(arg_keys[4], (MODEL_WIDTH, KEY_VALUE_HEADS * HEAD_SIZE), MODEL_WIDTH ** -0.5, 0.09375, ((0, 16),)),
        "value_weight": noise(arg_keys[5], (MODEL_WIDTH, KEY_VALUE_HEADS * HEAD_SIZE), MODEL_WIDTH ** -0.5, 0.09375, ((0, 16),)),
    }


rope_base = 500000.0 * 16.0 ** (128.0 / 126.0)
masked_score = -1.0e30


def apply_rotation(values, token_positions, head_count):
    head_width = values.shape[-1] // head_count
    half_width = head_width // 2
    freq_index = jnp.arange(half_width, dtype=jnp.float32)
    inverse = jnp.exp(-(2.0 * freq_index / head_width) * jnp.log(jnp.float32(rope_base)))
    angles = token_positions.astype(jnp.float32)[:, None] * inverse[None, :]
    cosine = jnp.cos(angles)[:, None, :]
    sine_table = jnp.sin(angles)[:, None, :]
    shaped = values.reshape(values.shape[0], head_count, head_width)
    front_half = shaped[..., :half_width]
    back_half = shaped[..., half_width:]
    turned = jnp.concatenate([front_half * cosine - back_half * sine_table, back_half * cosine + front_half * sine_table], axis=-1)
    return turned.reshape(values.shape[0], head_count * head_width)


def attend_block(query_block_rows, key_span_rows, value_span_rows, allowed):
    total_row_count = query_block_rows.shape[0]
    window_key_count = key_span_rows.shape[0]
    query_group_width = QUERY_HEADS // KEY_VALUE_HEADS
    query_heads_view = query_block_rows.astype(jnp.float32).reshape(total_row_count, KEY_VALUE_HEADS, query_group_width, HEAD_SIZE)
    key_heads_view = key_span_rows.astype(jnp.float32).reshape(window_key_count, KEY_VALUE_HEADS, HEAD_SIZE)
    value_heads_view = value_span_rows.astype(jnp.float32).reshape(window_key_count, KEY_VALUE_HEADS, HEAD_SIZE)
    scores = jnp.einsum("rhgd,khd->hgrk", query_heads_view, key_heads_view) * (HEAD_SIZE ** -0.5)
    scores = jnp.where(allowed[None, None], scores, masked_score)
    largest = jnp.max(scores, axis=-1, keepdims=True)
    expo_terms = jnp.exp(scores - largest)
    denominator = jnp.sum(expo_terms, axis=-1, keepdims=True)
    weights = (expo_terms / denominator).astype(jnp.bfloat16)
    mixed = jnp.einsum("hgrk,khd->rhgd", weights.astype(jnp.float32), value_heads_view)
    return mixed.reshape(total_row_count, QUERY_HEADS * HEAD_SIZE).astype(jnp.bfloat16)


def reference(hidden, dest, doc_ids, w_query, key_weight, value_weight):
    ordered = jnp.zeros_like(hidden).at[dest].set(hidden)
    query_raw = jnp.dot(ordered, w_query, preferred_element_type=jnp.float32).astype(jnp.bfloat16)
    key_unrotated = jnp.dot(ordered, key_weight, preferred_element_type=jnp.float32).astype(jnp.bfloat16)
    value_matrix = jnp.dot(ordered, value_weight, preferred_element_type=jnp.float32).astype(jnp.bfloat16)
    token_positions = jnp.arange(SEQ, dtype=jnp.int32)
    queries = apply_rotation(query_raw.astype(jnp.float32), token_positions, QUERY_HEADS).astype(jnp.bfloat16)
    key_matrix = apply_rotation(key_unrotated.astype(jnp.float32), token_positions, KEY_VALUE_HEADS).astype(jnp.bfloat16)
    padded_keys = jnp.concatenate([jnp.zeros((BLOCK_TOKENS, KEY_VALUE_HEADS * HEAD_SIZE), jnp.bfloat16), key_matrix], axis=0)
    padded_values = jnp.concatenate([jnp.zeros((BLOCK_TOKENS, KEY_VALUE_HEADS * HEAD_SIZE), jnp.bfloat16), value_matrix], axis=0)
    pad_docs = jnp.concatenate([jnp.full((BLOCK_TOKENS,), -1, jnp.int32), doc_ids.astype(jnp.int32)], axis=0)
    local_index = jnp.arange(BLOCK_TOKENS, dtype=jnp.int32)
    across = jnp.arange(2 * BLOCK_TOKENS, dtype=jnp.int32)
    reach = (across[None, :] > local_index[:, None]) & (across[None, :] <= local_index[:, None] + BLOCK_TOKENS)

    def one_block(block):
        start = (block * BLOCK_TOKENS).astype(jnp.int32)
        query_block_rows = lax.dynamic_slice_in_dim(queries, start, BLOCK_TOKENS, 0)
        key_span_rows = lax.dynamic_slice_in_dim(padded_keys, start, 2 * BLOCK_TOKENS, 0)
        value_span_rows = lax.dynamic_slice_in_dim(padded_values, start, 2 * BLOCK_TOKENS, 0)
        query_docs = lax.dynamic_slice_in_dim(pad_docs, start + BLOCK_TOKENS, BLOCK_TOKENS, 0)
        key_docs = lax.dynamic_slice_in_dim(pad_docs, start, 2 * BLOCK_TOKENS, 0)
        allowed = reach & (query_docs[:, None] == key_docs[None, :])
        return attend_block(query_block_rows, key_span_rows, value_span_rows, allowed)

    blocks = lax.map(one_block, jnp.arange(N_CTX, dtype=jnp.int32))
    return blocks.reshape(SEQ, QUERY_HEADS * HEAD_SIZE)
```

```python
import functools

import jax
import jax.numpy as jnp
from jax import lax
from jax.experimental import pallas as pl
from jax.experimental.pallas import tpu as pltpu
from jax.sharding import PartitionSpec as P

HEAD = 128
BLOCK = 512
CHIPS = 8
CHUNKS = 6
WIDE = 256
SLOTS = 256
WINDOW = 640
MESH = pl.DeviceIdType.MESH
rope_base = 500000.0 * 16.0 ** (128.0 / 126.0)
SCORE = HEAD**-0.5 * 1.4426950408889634
F32, BF16 = jnp.float32, jnp.bfloat16


def kernel(
    hid, dest, docs, cos, sin, wq, wk, wv, out,
    x_all, w_all, dests, pack, unpack, meta_s, meta_r, qkv, snd, rcv, keys, vals, qs, outs, bias,
    one, six,
):
    dp, cx = lax.axis_index("dp"), lax.axis_index("ctx")
    z, xh = dp // 2, lax.rem(dp, 2)
    xl, y, core = cx // 8, lax.rem(cx // 2, 4), lax.rem(cx, 2)
    chip, half = cx // 2, lax.rem(z, 2)
    other = 1 - core

    def at_y(step):
        return lax.rem(y + step, 4)

    sibling = (dp, chip * 2 + other)
    inner = (dp, (1 - xl) * 8 + y * 2 + core)
    outer = (z * 2 + 1 - xh, (1 - xl) * 8 + y * 2 + core)
    above = (lax.rem(z + 1, 4) * 2 + xh, cx)
    below = (lax.rem(z + 3, 4) * 2 + xh, cx)

    def peer(step):
        return lax.rem(chip + step, CHIPS)

    (hid_l, hid_s, hid_r, dst_s, dst_r, met_s, met_r) = (one.at[i] for i in range(7))
    (w_l, w_s, w_r, y_s, y_r, x_s, x_r, z_s, z_r, a_s, a_r, h_s, h_r, o_l, o_s, o_r) = (
        six.at[i] for i in range(16)
    )

    barrier = pltpu.get_barrier_semaphore()
    near = [sibling, outer, above, below] + [(dp, peer(r) * 2 + core) for r in range(1, CHIPS)]
    for device in near:
        pl.semaphore_signal(barrier, inc=1, device_id=device, device_id_type=MESH)
    pl.semaphore_wait(barrier, len(near))

    def remote(src, dst, s, r, device):
        return pltpu.make_async_remote_copy(
            src_ref=src, dst_ref=dst, send_sem=s, recv_sem=r, device_id=device, device_id_type=MESH
        )

    def drain(ref, sem):
        pltpu.make_async_copy(ref, ref, sem).wait()

    def columns(k, of):
        if k == 0:
            return wk.at[:, pl.ds(pl.multiple_of(of * WIDE, WIDE), WIDE)]
        if k == 1:
            return wv.at[:, pl.ds(pl.multiple_of(of * WIDE, WIDE), WIDE)]
        return wq.at[:, pl.ds(pl.multiple_of(of * 1024 + (k - 2) * WIDE, WIDE), WIDE)]

    mine = pl.ds(pl.multiple_of(core * 256, 256), 256)
    my_rows = pl.ds(pl.multiple_of(core * BLOCK, BLOCK), BLOCK)
    for k in range(CHUNKS):
        spot = w_all.at[k, chip, mine]
        remote(columns(k, other), spot, w_s.at[k], w_r.at[k], sibling).start()
        pltpu.make_async_copy(columns(k, core), spot, w_l.at[k]).start()
    dests[core] = jnp.broadcast_to(dest[...], (8, BLOCK))
    remote(dests.at[core], dests.at[core], dst_s, dst_r, sibling).start()
    remote(hid, x_all.at[my_rows], hid_s, hid_r, sibling).start()
    pltpu.make_async_copy(hid, x_all.at[my_rows], hid_l).start()

    sent_half = pl.ds(pl.multiple_of(half * 256, 256), 256)
    low = pl.ds(pl.multiple_of(half * 256, 128), 128)
    high = pl.ds(pl.multiple_of(half * 256 + 128, 128), 128)

    def stage_y(k):
        own = w_all.at[k, chip, mine]
        drain(own, w_l.at[k])
        drain(own, w_r.at[k])
        spot = w_all.at[k, chip, sent_half]
        for step in (1, 3, 2):
            remote(spot, spot, y_s.at[k], y_r.at[k], (dp, xl * 8 + at_y(step) * 2 + core)).start()
        remote(spot, spot, x_s.at[k], x_r.at[k], inner).start()

    def to_z(k, shard):
        spot = w_all.at[k, shard, low]
        remote(spot, spot, z_s.at[k], z_r.at[k], below).start()
        spot = w_all.at[k, shard, high]
        remote(spot, spot, z_s.at[k], z_r.at[k], above).start()

    def pieces(k, n):
        return w_all.at[k, pl.ds(0, n), pl.ds(0, 256)]

    def stage_x(k):
        drain(pieces(k, 3), y_r.at[k])
        for step in (1, 3, 2):
            spot = w_all.at[k, xl * 4 + at_y(step), sent_half]
            remote(spot, spot, x_s.at[k], x_r.at[k], outer).start()
        for step in (1, 3, 2):
            to_z(k, xl * 4 + at_y(step))

    def stage_z(k):
        drain(pieces(k, 4), x_r.at[k])
        for step in range(4):
            to_z(k, (1 - xl) * 4 + at_y(step))

    def project(k):
        drain(pieces(k, 7), z_r.at[k])

        def rows(m, _):
            at = pl.ds(pl.multiple_of(m * 512, 512), 512)
            qkv[at, :] = jnp.dot(
                x_all[at, :], w_all[k].reshape(CHIPS * 512, WIDE), preferred_element_type=F32
            ).astype(BF16)
            return 0

        lax.fori_loop(0, 2, rows, 0)

        def send(r, _):
            j = peer(r)
            snd[k, j] = jnp.dot(
                pack[pl.ds(pl.multiple_of(j * SLOTS, SLOTS), SLOTS), :], qkv[...],
                preferred_element_type=F32,
            ).astype(BF16)
            remote(
                snd.at[k, j], rcv.at[k, chip], a_s.at[k], a_r.at[k], (dp, j * 2 + core)
            ).start()
            return 0

        lax.fori_loop(1, CHIPS, send, 0)
        rcv[k, chip] = jnp.dot(
            pack[pl.ds(pl.multiple_of(chip * SLOTS, SLOTS), SLOTS), :], qkv[...],
            preferred_element_type=F32,
        ).astype(BF16)

    def placed(k, t):
        got = rcv[k, :, pl.ds(pl.multiple_of(t * 128, 128), 128), :].reshape(CHIPS * 128, WIDE)
        return jnp.dot(unpack[t], got, preferred_element_type=F32)

    def turned(v, t):
        at = pl.ds(pl.multiple_of(t * BLOCK, BLOCK), BLOCK)
        return (v * cos[at, :] + pltpu.roll(v, 64, 1) * sin[at, :]).astype(BF16)

    following = (dp, peer(1) * 2 + core)

    def halo(ref, i):
        remote(
            ref.at[:, pl.ds(1024, 512)], ref.at[:, pl.ds(0, 512)], h_s.at[i], h_r.at[i], following
        ).start()

    def receive(k):
        drain(rcv.at[k, pl.ds(0, 7)], a_r.at[k])

        def block(t, _):
            v = placed(k, t)
            for h in range(2):
                head = v[:, h * HEAD : (h + 1) * HEAD]

                @pl.when(k == 0)
                def _():
                    keys[h, pl.ds(pl.multiple_of(512 + t * 512, 512), 512), :] = turned(head, t)

                @pl.when(k == 1)
                def _():
                    vals[h, pl.ds(pl.multiple_of(512 + t * 512, 512), 512), :] = head.astype(BF16)

                @pl.when(k >= 2)
                def _():
                    qs[h, pl.ds(pl.multiple_of(t * 512, 512), 512), :] = turned(head, t)

            return 0

        lax.fori_loop(0, 2, block, 0)

        @pl.when(k == 0)
        def _():
            halo(keys, 0)

        @pl.when(k == 1)
        def _():
            halo(vals, 1)

        @pl.when(k == 2)
        def _():
            drain(keys.at[:, pl.ds(0, 512)], h_r.at[0])
            drain(vals.at[:, pl.ds(0, 512)], h_r.at[1])

        @pl.when(k >= 2)
        def _():
            attend(k - 2)

    def attend(c):
        g = c // 2

        def tile(i, _):
            at = pl.multiple_of(i * 128, 128)
            q = qs[:, pl.ds(at, 128), :].reshape(256, HEAD)
            s = lax.dot_general(
                q, keys[g, pl.ds(at, WINDOW), :], (((1,), (1,)), ((), ())),
                preferred_element_type=F32,
            )
            s = s.reshape(2, 128, WINDOW) * SCORE + bias[i][None]
            s = s.reshape(256, WINDOW)
            e = jnp.exp2(s - jnp.max(s, axis=1, keepdims=True))
            total = jnp.sum(e, axis=1, keepdims=True)
            o = jnp.dot(e.astype(BF16), vals[g, pl.ds(at, WINDOW), :], preferred_element_type=F32)
            o = (o / total).astype(BF16)
            to = pl.ds(pl.multiple_of(lax.rem(i, 4) * 128, 128), 128)
            outs[i // 4, c, to, pl.ds(0, HEAD)] = o[:128]
            outs[i // 4, c, to, pl.ds(HEAD, HEAD)] = o[128:]
            return 0

        lax.fori_loop(0, 8, tile, 0)
        spot = out.at[:, pl.ds(pl.multiple_of(core * 1024 + c * WIDE, WIDE), WIDE)]
        remote(outs.at[other, c], spot, o_s.at[c], o_r.at[c], sibling).start()
        pltpu.make_async_copy(outs.at[core, c], spot, o_l.at[c]).start()

    stage_y(0)
    stage_y(1)

    drain(dests.at[core], dst_r)
    tri = (
        lax.broadcasted_iota(jnp.int32, (BLOCK, BLOCK), 0)
        <= lax.broadcasted_iota(jnp.int32, (BLOCK, BLOCK), 1)
    ).astype(BF16)
    targets = jnp.zeros((8, CHIPS * SLOTS), F32)
    for b in range(2):
        d = dests[b][:1]
        owner = lax.shift_right_logical(d, 9)
        hits = lax.broadcasted_iota(jnp.int32, (16, BLOCK), 0) == owner
        counts = jnp.dot(hits.astype(BF16), tri, preferred_element_type=F32)
        rank = jnp.sum(jnp.where(hits, counts, 0.0), axis=0, keepdims=True) - 1.0
        slot = (owner * 2 + b) * 64 + rank.astype(jnp.int32)

        def fill(m, _):
            at = pl.multiple_of(m * 256, 256)
            pack[pl.ds(at, 256), pl.ds(b * BLOCK, BLOCK)] = (
                lax.broadcasted_iota(jnp.int32, (256, BLOCK), 0) + at == slot
            ).astype(BF16)
            return 0

        lax.fori_loop(0, 8, fill, 0)
        target = jnp.bitwise_and(d, 511) + 1
        row = lax.broadcasted_iota(jnp.int32, (8, BLOCK), 0)
        digits = jnp.where(
            row == 0,
            lax.shift_right_logical(target, 5),
            jnp.where(row == 1, jnp.bitwise_and(target, 31), 0),
        )
        targets = targets + lax.dot_general(
            digits.astype(F32).astype(BF16), pack[:, b * BLOCK : (b + 1) * BLOCK],
            (((1,), (1,)), ((), ())), preferred_element_type=F32,
        )
    targets = targets[:1] * 32.0 + targets[1:2]
    for j in range(CHIPS):
        for t in range(2):
            at = (j * 2 + t) * 128
            meta_s[j, t : t + 1, :] = targets[:, at : at + 128]
        meta_s[j, 2:8, :] = jnp.zeros((6, 128), F32)
    for r in range(1, CHIPS):
        j = peer(r)
        remote(meta_s.at[j], meta_r.at[chip], met_s, met_r, (dp, j * 2 + core)).start()
    meta_r[chip] = meta_s[chip]

    stage_x(0)

    def mask(i, _):
        at = pl.multiple_of(i * 128, 128)
        own = docs[:, pl.ds(pl.multiple_of(at + 512, 128), 128)].astype(F32)
        own = jnp.transpose(jnp.broadcast_to(own, (128, 128)))[:, :1]
        row = lax.broadcasted_iota(jnp.int32, (128, WINDOW), 0)
        col = lax.broadcasted_iota(jnp.int32, (128, WINDOW), 1)
        seen = (col > row) & (col <= row + 512)
        seen = seen & (own == docs[:, pl.ds(at, WINDOW)].astype(F32))
        bias[i] = jnp.where(seen, 0.0, -1e30)
        return 0

    lax.fori_loop(0, 8, mask, 0)

    stage_y(2)
    stage_x(1)
    stage_z(0)

    drain(meta_r.at[pl.ds(0, 7)], met_r)
    place = lax.broadcasted_iota(jnp.int32, (BLOCK, 128), 0).astype(F32) + 1.0
    for t in range(2):
        for i in range(CHIPS):
            unpack[t, :, i * 128 : (i + 1) * 128] = (place == meta_r[i, t : t + 1, :]).astype(BF16)

    drain(x_all.at[my_rows], hid_l)
    drain(x_all.at[my_rows], hid_r)

    def step(i, _):
        @pl.when(i < CHUNKS - 3)
        def _():
            stage_y(i + 3)

        @pl.when(i < CHUNKS - 2)
        def _():
            stage_x(i + 2)

        @pl.when(i < CHUNKS - 1)
        def _():
            stage_z(i + 1)

        @pl.when(i < CHUNKS)
        def _():
            project(i)

        @pl.when(i >= 1)
        def _():
            receive(i - 1)

        return 0

    lax.fori_loop(0, CHUNKS + 1, step, 0)

    for c in range(4):
        spot = out.at[:, pl.ds(c * WIDE, WIDE)]
        drain(spot, o_l.at[c])
        drain(spot, o_r.at[c])
        drain(outs.at[0, c], o_s.at[c])
    for k in range(CHUNKS):
        drain(pieces(k, 1), w_s.at[k])
        drain(pieces(k, 3), y_s.at[k])
        drain(pieces(k, 4), x_s.at[k])
        drain(pieces(k, 7), z_s.at[k])
        drain(snd.at[k, pl.ds(0, 7)], a_s.at[k])
    drain(keys.at[:, pl.ds(0, 512)], h_s.at[0])
    drain(vals.at[:, pl.ds(0, 512)], h_s.at[1])
    drain(x_all.at[my_rows], hid_s)
    drain(dests.at[core], dst_s)
    drain(meta_s.at[pl.ds(0, 7)], met_s)


def on_device(hidden, dest, doc_ids, w_query, key_weight, value_weight):
    chip = lax.axis_index("ctx") // 2
    positions = (chip * 1024 + jnp.arange(1024, dtype=jnp.int32)).astype(F32)
    freq = jnp.arange(HEAD // 2, dtype=F32)
    inverse = jnp.exp(-(2.0 * freq / HEAD) * jnp.log(F32(rope_base)))
    angles = positions[:, None] * inverse[None, :]
    cosine, sine = jnp.cos(angles), jnp.sin(angles)
    cosine = jnp.concatenate([cosine, cosine], axis=1)
    sine = jnp.concatenate([-sine, sine], axis=1)
    docs = jnp.concatenate([jnp.full((BLOCK,), -1, jnp.int32), doc_ids])
    docs = lax.dynamic_slice_in_dim(docs, chip * 1024, 1536, 0).reshape(1, 1536)
    anywhere = pl.BlockSpec(memory_space=pl.ANY)
    local = pl.BlockSpec(memory_space=pltpu.VMEM)
    return pl.pallas_call(
        kernel,
        out_shape=jax.ShapeDtypeStruct((BLOCK, 2048), BF16),
        in_specs=[anywhere, local, local, local, local, anywhere, anywhere, anywhere],
        out_specs=anywhere,
        scratch_shapes=[
            pltpu.VMEM((1024, 4096), BF16),
            pltpu.VMEM((CHUNKS, CHIPS, 512, WIDE), BF16),
            pltpu.VMEM((2, 8, BLOCK), jnp.int32),
            pltpu.VMEM((CHIPS * SLOTS, 1024), BF16),
            pltpu.VMEM((2, BLOCK, 1024), BF16),
            pltpu.VMEM((CHIPS, 8, 128), F32),
            pltpu.VMEM((CHIPS, 8, 128), F32),
            pltpu.VMEM((1024, WIDE), BF16),
            pltpu.VMEM((CHUNKS, CHIPS, SLOTS, WIDE), BF16),
            pltpu.VMEM((CHUNKS, CHIPS, SLOTS, WIDE), BF16),
            pltpu.VMEM((2, 1536, HEAD), BF16),
            pltpu.VMEM((2, 1536, HEAD), BF16),
            pltpu.VMEM((2, 1024, HEAD), BF16),
            pltpu.VMEM((2, 4, BLOCK, WIDE), BF16),
            pltpu.VMEM((8, 128, WINDOW), F32),
            pltpu.SemaphoreType.DMA((7,)),
            pltpu.SemaphoreType.DMA((16, CHUNKS)),
        ],
        compiler_params=pltpu.CompilerParams(
            collective_id=0, has_side_effects=True, vmem_limit_bytes=60 * 2**20
        ),
    )(hidden, dest.reshape(1, BLOCK), docs, cosine, sine, w_query, key_weight, value_weight)


def solution(mesh):
    placed = (
        P(("dp", "ctx"), None),
        P(("dp", "ctx")),
        P("dp"),
        P("ctx", None),
        P("ctx", None),
        P("ctx", None),
    )
    return jax.shard_map(
        on_device, mesh=mesh, in_specs=placed, out_specs=P(("dp", "ctx"), None), check_vma=False
    )
```

```python
import jax
import jax.numpy as jnp
import numpy as np
from jax import lax
from jax.experimental import pallas as pl
from jax.experimental.pallas import tpu as pltpu
from jax.sharding import PartitionSpec as P

HEAD = 128
BLOCK = 512
CHIPS = 8
CHUNKS = 6
WIDE = 256
SLOTS = 256
WINDOW = 640
MESH = pl.DeviceIdType.MESH
rope_base = 500000.0 * 16.0 ** (128.0 / 126.0)
SCORE = HEAD**-0.5 * 1.4426950408889634
F32, BF16 = jnp.float32, jnp.bfloat16
QUARTERS = (False, False, True, True, True, True)


def angles():
    inverse = rope_base ** (-2.0 * np.arange(64) / HEAD)
    steps = [np.arange(8) * 1024, np.arange(32) * 32, np.arange(32)]
    parts = []
    for at in steps:
        angle = at[:, None] * inverse[None, :]
        parts += [np.tile(np.cos(angle), (1, 2)), np.tile(np.sin(angle), (1, 2))]
    return np.concatenate(parts).astype(np.float32)


def kernel(
    hid, dest, docs, table, wq, wk, wv, out,
    cos, sin, turn, x_all, w_all, dests, pack, unpack, meta_s, meta_r, qkv, snd, rcv, keys, vals, qs, outs, bias,
    one, six,
):
    dp, cx = lax.axis_index("dp"), lax.axis_index("ctx")
    z, xh = dp // 2, lax.rem(dp, 2)
    xl, y, core = cx // 8, lax.rem(cx // 2, 4), lax.rem(cx, 2)
    chip, half = cx // 2, lax.rem(z, 2)
    other = 1 - core

    def at_y(step):
        return lax.rem(y + step, 4)

    sibling = (dp, chip * 2 + other)
    inner = (dp, (1 - xl) * 8 + y * 2 + core)
    outer = (z * 2 + 1 - xh, (1 - xl) * 8 + y * 2 + core)
    above = (lax.rem(z + 1, 4) * 2 + xh, cx)
    below = (lax.rem(z + 3, 4) * 2 + xh, cx)

    def peer(step):
        return lax.rem(chip + step, CHIPS)

    (hid_l, hid_s, hid_r, dst_s, dst_r, met_s, met_r) = (one.at[i] for i in range(7))
    (w_l, w_s, w_r, y_s, y_r, x_s, x_r, z_s, z_r, a_s, a_r, h_s, h_r, o_l, o_s, o_r, f_s, f_r) = (
        six.at[i] for i in range(18)
    )

    barrier = pltpu.get_barrier_semaphore()
    near = [sibling, outer, above, below] + [(dp, peer(r) * 2 + core) for r in range(1, CHIPS)]
    for device in near:
        pl.semaphore_signal(barrier, inc=1, device_id=device, device_id_type=MESH)
    pl.semaphore_wait(barrier, len(near))

    def remote(src, dst, s, r, device):
        return pltpu.make_async_remote_copy(
            src_ref=src, dst_ref=dst, send_sem=s, recv_sem=r, device_id=device, device_id_type=MESH
        )

    def drain(ref, sem):
        pltpu.make_async_copy(ref, ref, sem).wait()

    def columns(k, of):
        if k == 0:
            return wk.at[:, pl.ds(pl.multiple_of(of * WIDE, WIDE), WIDE)]
        if k == 1:
            return wv.at[:, pl.ds(pl.multiple_of(of * WIDE, WIDE), WIDE)]
        return wq.at[:, pl.ds(pl.multiple_of(of * 1024 + (k - 2) * WIDE, WIDE), WIDE)]

    mine = pl.ds(pl.multiple_of(core * 256, 256), 256)
    my_rows = pl.ds(pl.multiple_of(core * BLOCK, BLOCK), BLOCK)
    for k in range(CHUNKS):
        spot = w_all.at[k, 0, mine]
        remote(columns(k, other), spot, w_s.at[k], w_r.at[k], sibling).start()
        pltpu.make_async_copy(columns(k, core), spot, w_l.at[k]).start()
    dests[core] = jnp.broadcast_to(dest[...], (8, BLOCK))
    remote(dests.at[core], dests.at[core], dst_s, dst_r, sibling).start()

    def run(start, size):
        return pl.ds(pl.multiple_of(start, size), size)

    def part(k, shards):
        rows = run(z * 128, 128) if QUARTERS[k] else run(half * 256, 256)
        return w_all.at[k, shards, rows]

    def shape(k, n, rows):
        return w_all.at[k, pl.ds(0, n), pl.ds(0, rows)]

    def width(k):
        return 128 if QUARTERS[k] else 256

    def stage_y(k):
        own = w_all.at[k, 0, mine]
        drain(own, w_l.at[k])
        drain(own, w_r.at[k])
        for step in (1, 3, 2):
            remote(
                part(k, 0), part(k, 4 - step), y_s.at[k], y_r.at[k],
                (dp, xl * 8 + at_y(step) * 2 + core),
            ).start()
        remote(
            part(k, 0), part(k, 4), x_s.at[k], x_r.at[k], outer if QUARTERS[k] else inner
        ).start()

    def to_z(k, shards):
        for i, device in enumerate((below, above)):
            if QUARTERS[k]:
                spot = part(k, shards)
            else:
                spot = w_all.at[k, shards, run(half * 256 + i * 128, 128)]
            remote(spot, spot, z_s.at[k], z_r.at[k], device).start()

    def stage_x(k):
        drain(shape(k, 3, width(k)), y_r.at[k])
        remote(
            part(k, pl.ds(1, 3)), part(k, pl.ds(5, 3)), x_s.at[k], x_r.at[k], outer
        ).start()
        to_z(k, pl.ds(1, 3))

    def stage_z(k):
        drain(shape(k, 4, width(k)), x_r.at[k])
        to_z(k, pl.ds(4, 4))

    def stage_f(k):
        if QUARTERS[k]:
            drain(shape(k, 7, 256), z_r.at[k])
            spot = w_all.at[k, pl.ds(1, 7), run(lax.rem(z + 3, 4) * 128, 64)]
            remote(spot, spot, f_s.at[k], f_r.at[k], above).start()
            spot = w_all.at[k, pl.ds(1, 7), run(lax.rem(z + 1, 4) * 128 + 64, 64)]
            remote(spot, spot, f_s.at[k], f_r.at[k], below).start()

    def arrived(k):
        if QUARTERS[k]:
            drain(shape(k, 7, 128), f_r.at[k])
        else:
            drain(shape(k, 7, 256), z_r.at[k])

    def at_step(i, late, stage):
        for k in range(max(late, 0), CHUNKS):
            pl.when(i == k - late)(lambda k=k: stage(k))

    def project(k):
        at_step(k, 0, arrived)

        def rows(m, _):
            at = pl.ds(pl.multiple_of(m * 512, 512), 512)
            qkv[at, :] = jnp.dot(
                x_all[at, :], w_all[k].reshape(CHIPS * 512, WIDE), preferred_element_type=F32
            ).astype(BF16)
            return 0

        lax.fori_loop(0, 2, rows, 0)

        def send(r, _):
            j = peer(r)
            snd[k, j] = jnp.dot(
                pack[pl.ds(pl.multiple_of(j * SLOTS, SLOTS), SLOTS), :], qkv[...],
                preferred_element_type=F32,
            ).astype(BF16)
            remote(
                snd.at[k, j], rcv.at[k, chip], a_s.at[k], a_r.at[k], (dp, j * 2 + core)
            ).start()
            return 0

        lax.fori_loop(1, CHIPS, send, 0)
        rcv[k, chip] = jnp.dot(
            pack[pl.ds(pl.multiple_of(chip * SLOTS, SLOTS), SLOTS), :], qkv[...],
            preferred_element_type=F32,
        ).astype(BF16)

    def placed(k, t):
        got = rcv[k, :, pl.ds(pl.multiple_of(t * 128, 128), 128), :].reshape(CHIPS * 128, WIDE)
        return jnp.dot(unpack[t], got, preferred_element_type=F32)

    def turned(v, t):
        at = pl.ds(pl.multiple_of(t * BLOCK, BLOCK), BLOCK)
        return (v * cos[at, :] + pltpu.roll(v, 64, 1) * sin[at, :]).astype(BF16)

    following = (dp, peer(1) * 2 + core)

    def halo(ref, i):
        remote(
            ref.at[:, pl.ds(1024, 512)], ref.at[:, pl.ds(0, 512)], h_s.at[i], h_r.at[i], following
        ).start()

    def receive(k):
        drain(rcv.at[k, pl.ds(0, 7)], a_r.at[k])

        def block(t, _):
            v = placed(k, t)
            for h in range(2):
                head = v[:, h * HEAD : (h + 1) * HEAD]

                @pl.when(k == 0)
                def _():
                    keys[h, pl.ds(pl.multiple_of(512 + t * 512, 512), 512), :] = turned(head, t)

                @pl.when(k == 1)
                def _():
                    vals[h, pl.ds(pl.multiple_of(512 + t * 512, 512), 512), :] = head.astype(BF16)

                @pl.when(k >= 2)
                def _():
                    qs[h, pl.ds(pl.multiple_of(t * 512, 512), 512), :] = turned(head, t)

            return 0

        lax.fori_loop(0, 2, block, 0)

        @pl.when(k == 0)
        def _():
            halo(keys, 0)

        @pl.when(k == 1)
        def _():
            halo(vals, 1)

        @pl.when(k == 2)
        def _():
            drain(keys.at[:, pl.ds(0, 512)], h_r.at[0])
            drain(vals.at[:, pl.ds(0, 512)], h_r.at[1])

        @pl.when(k >= 2)
        def _():
            attend(k - 2)

    def attend(c):
        g = c // 2

        def tile(i, _):
            at = pl.multiple_of(i * 128, 128)
            q = qs[:, pl.ds(at, 128), :].reshape(256, HEAD)
            s = lax.dot_general(
                q, keys[g, pl.ds(at, WINDOW), :], (((1,), (1,)), ((), ())),
                preferred_element_type=F32,
            )
            s = s.reshape(2, 128, WINDOW) * SCORE + bias[i][None]
            s = s.reshape(256, WINDOW)
            e = jnp.exp2(s - jnp.max(s, axis=1, keepdims=True))
            total = jnp.sum(e, axis=1, keepdims=True)
            o = jnp.dot(e.astype(BF16), vals[g, pl.ds(at, WINDOW), :], preferred_element_type=F32)
            o = (o / total).astype(BF16)
            to = pl.ds(pl.multiple_of(lax.rem(i, 4) * 128, 128), 128)
            outs[i // 4, c, to, pl.ds(0, HEAD)] = o[:128]
            outs[i // 4, c, to, pl.ds(HEAD, HEAD)] = o[128:]
            return 0

        lax.fori_loop(0, 8, tile, 0)
        spot = out.at[:, pl.ds(pl.multiple_of(core * 1024 + c * WIDE, WIDE), WIDE)]
        remote(outs.at[other, c], spot, o_s.at[c], o_r.at[c], sibling).start()
        pltpu.make_async_copy(outs.at[core, c], spot, o_l.at[c]).start()

    stage_y(0)
    stage_y(1)
    for r in range(CHIPS):
        shard = (xl if r < 4 else 1 - xl) * 4 + at_y(r % 4)
        src = hid.at[:, run(shard * 512, 512)]
        spot = x_all.at[my_rows, pl.ds(r * 512, 512)]
        remote(src, spot, hid_s, hid_r, sibling).start()
        pltpu.make_async_copy(src, spot, hid_l).start()
    for k in range(2, CHUNKS):
        stage_y(k)

    drain(dests.at[core], dst_r)
    tri = (
        lax.broadcasted_iota(jnp.int32, (BLOCK, BLOCK), 0)
        <= lax.broadcasted_iota(jnp.int32, (BLOCK, BLOCK), 1)
    ).astype(BF16)
    targets = jnp.zeros((8, CHIPS * SLOTS), F32)
    for b in range(2):
        d = dests[b][:1]
        owner = lax.shift_right_logical(d, 9)
        hits = lax.broadcasted_iota(jnp.int32, (16, BLOCK), 0) == owner
        counts = jnp.dot(hits.astype(BF16), tri, preferred_element_type=F32)
        rank = jnp.sum(jnp.where(hits, counts, 0.0), axis=0, keepdims=True) - 1.0
        slot = (owner * 2 + b) * 64 + rank.astype(jnp.int32)

        def fill(m, _):
            at = pl.multiple_of(m * 256, 256)
            pack[pl.ds(at, 256), pl.ds(b * BLOCK, BLOCK)] = (
                lax.broadcasted_iota(jnp.int32, (256, BLOCK), 0) + at == slot
            ).astype(BF16)
            return 0

        lax.fori_loop(0, 8, fill, 0)
        target = jnp.bitwise_and(d, 511) + 1
        row = lax.broadcasted_iota(jnp.int32, (8, BLOCK), 0)
        digits = jnp.where(
            row == 0,
            lax.shift_right_logical(target, 5),
            jnp.where(row == 1, jnp.bitwise_and(target, 31), 0),
        )
        targets = targets + lax.dot_general(
            digits.astype(F32).astype(BF16), pack[:, b * BLOCK : (b + 1) * BLOCK],
            (((1,), (1,)), ((), ())), preferred_element_type=F32,
        )
    targets = targets[:1] * 32.0 + targets[1:2]
    for j in range(CHIPS):
        for t in range(2):
            at = (j * 2 + t) * 128
            meta_s[j, t : t + 1, :] = targets[:, at : at + 128]
        meta_s[j, 2:8, :] = jnp.zeros((6, 128), F32)
    for r in range(1, CHIPS):
        j = peer(r)
        remote(meta_s.at[j], meta_r.at[chip], met_s, met_r, (dp, j * 2 + core)).start()
    meta_r[chip] = meta_s[chip]

    stage_x(0)

    def mask(i, _):
        def doc(at):
            line = docs[pl.ds(jnp.maximum(at, 0), 1), :].astype(F32)
            return jnp.where(at >= 0, line, -1.0)

        own = jnp.transpose(jnp.broadcast_to(doc(chip * 8 + i), (128, 128)))
        row = lax.broadcasted_iota(jnp.int32, (128, 128), 0)
        for j in range(5):
            col = lax.broadcasted_iota(jnp.int32, (128, 128), 1) + j * 128
            seen = (col > row) & (col <= row + 512) & (own == doc(chip * 8 - 4 + i + j))
            bias[i, :, j * 128 : (j + 1) * 128] = jnp.where(seen, 0.0, -1e30)
        return 0

    lax.fori_loop(0, 8, mask, 0)

    stage_x(1)
    stage_z(0)

    cc, cs = table[pl.ds(chip, 1), :], table[pl.ds(8 + chip, 1), :]
    turn[0] = table[16:48, :] * cc - table[48:80, :] * cs
    turn[1] = table[48:80, :] * cc + table[16:48, :] * cs
    sign = jnp.where(lax.broadcasted_iota(jnp.int32, (1, HEAD), 1) < 64, -1.0, 1.0)

    def rotary(i, _):
        at = run(i * 32, 32)
        ca, sa = turn[0, pl.ds(i, 1), :], turn[1, pl.ds(i, 1), :]
        cos[at, :] = table[80:112, :] * ca - table[112:144, :] * sa
        sin[at, :] = (table[112:144, :] * ca + table[80:112, :] * sa) * sign
        return 0

    lax.fori_loop(0, 32, rotary, 0)

    stage_x(2)
    stage_z(1)

    drain(meta_r.at[pl.ds(0, 7)], met_r)
    place = lax.broadcasted_iota(jnp.int32, (BLOCK, 128), 0).astype(F32) + 1.0
    for t in range(2):
        for i in range(CHIPS):
            unpack[t, :, i * 128 : (i + 1) * 128] = (place == meta_r[i, t : t + 1, :]).astype(BF16)

    drain(x_all.at[my_rows], hid_l)
    drain(x_all.at[my_rows], hid_r)

    def step(i, _):
        @pl.when(i < CHUNKS)
        def _():
            project(i)

        at_step(i, 3, stage_x)
        at_step(i, 2, stage_z)
        at_step(i, 1, stage_f)

        @pl.when(i >= 1)
        def _():
            receive(i - 1)

        return 0

    lax.fori_loop(0, CHUNKS + 1, step, 0)

    for c in range(4):
        spot = out.at[:, pl.ds(c * WIDE, WIDE)]
        drain(spot, o_l.at[c])
        drain(spot, o_r.at[c])
        drain(outs.at[0, c], o_s.at[c])
    for k in range(CHUNKS):
        drain(shape(k, 1, 256), w_s.at[k])
        drain(shape(k, 3, width(k)), y_s.at[k])
        drain(shape(k, 4, width(k)), x_s.at[k])
        drain(shape(k, 7, 256), z_s.at[k])
        if QUARTERS[k]:
            drain(shape(k, 7, 128), f_s.at[k])
        drain(snd.at[k, pl.ds(0, 7)], a_s.at[k])
    drain(keys.at[:, pl.ds(0, 512)], h_s.at[0])
    drain(vals.at[:, pl.ds(0, 512)], h_s.at[1])
    drain(x_all.at[my_rows], hid_s)
    drain(dests.at[core], dst_s)
    drain(meta_s.at[pl.ds(0, 7)], met_s)


def on_device(hidden, dest, doc_ids, w_query, key_weight, value_weight):
    anywhere = pl.BlockSpec(memory_space=pl.ANY)
    local = pl.BlockSpec(memory_space=pltpu.VMEM)
    return pl.pallas_call(
        kernel,
        out_shape=jax.ShapeDtypeStruct((BLOCK, 2048), BF16),
        in_specs=[anywhere, local, local, local, anywhere, anywhere, anywhere],
        out_specs=anywhere,
        scratch_shapes=[
            pltpu.VMEM((1024, HEAD), F32),
            pltpu.VMEM((1024, HEAD), F32),
            pltpu.VMEM((2, 32, HEAD), F32),
            pltpu.VMEM((1024, 4096), BF16),
            pltpu.VMEM((CHUNKS, CHIPS, 512, WIDE), BF16),
            pltpu.VMEM((2, 8, BLOCK), jnp.int32),
            pltpu.VMEM((CHIPS * SLOTS, 1024), BF16),
            pltpu.VMEM((2, BLOCK, 1024), BF16),
            pltpu.VMEM((CHIPS, 8, 128), F32),
            pltpu.VMEM((CHIPS, 8, 128), F32),
            pltpu.VMEM((1024, WIDE), BF16),
            pltpu.VMEM((CHUNKS, CHIPS, SLOTS, WIDE), BF16),
            pltpu.VMEM((CHUNKS, CHIPS, SLOTS, WIDE), BF16),
            pltpu.VMEM((2, 1536, HEAD), BF16),
            pltpu.VMEM((2, 1536, HEAD), BF16),
            pltpu.VMEM((2, 1024, HEAD), BF16),
            pltpu.VMEM((2, 4, BLOCK, WIDE), BF16),
            pltpu.VMEM((8, 128, WINDOW), F32),
            pltpu.SemaphoreType.DMA((7,)),
            pltpu.SemaphoreType.DMA((18, CHUNKS)),
        ],
        compiler_params=pltpu.CompilerParams(
            collective_id=0, has_side_effects=True, vmem_limit_bytes=60 * 2**20
        ),
    )(
        hidden, dest.reshape(1, BLOCK), doc_ids.reshape(64, 128), jnp.asarray(angles()),
        w_query, key_weight, value_weight,
    )


def solution(mesh):
    placed = (
        P(("dp", "ctx"), None),
        P(("dp", "ctx")),
        P("dp"),
        P("ctx", None),
        P("ctx", None),
        P("ctx", None),
    )
    return jax.shard_map(
        on_device, mesh=mesh, in_specs=placed, out_specs=P(("dp", "ctx"), None), check_vma=False
    )
```

```python
import jax
import jax.numpy as jnp
import numpy as np
from jax import lax
from jax.experimental import pallas as pl
from jax.experimental.pallas import tpu as pltpu
from jax.sharding import PartitionSpec as P

HEAD = 128
BLOCK = 512
CHIPS = 8
CHUNKS = 6
WIDE = 256
SLOTS = 256
WINDOW = 640
MESH = pl.DeviceIdType.MESH
rope_base = 500000.0 * 16.0 ** (128.0 / 126.0)
SCORE = HEAD**-0.5 * 1.4426950408889634
F32, BF16 = jnp.float32, jnp.bfloat16
QUARTERS = (False, False, False, False, True, True)


def angles():
    inverse = rope_base ** (-2.0 * np.arange(64) / HEAD)
    steps = [np.arange(8) * 1024, np.arange(32) * 32, np.arange(32)]
    parts = []
    for at in steps:
        angle = at[:, None] * inverse[None, :]
        parts += [np.tile(np.cos(angle), (1, 2)), np.tile(np.sin(angle), (1, 2))]
    return np.concatenate(parts).astype(np.float32)


def kernel(
    hid, dest, docs, table, wq, wk, wv, out,
    cos, sin, turn, x_all, w_all, dests, pack, unpack, meta_s, meta_r, qkv, snd, rcv, keys, vals, qs, outs, bias,
    one, six,
):
    dp, cx = lax.axis_index("dp"), lax.axis_index("ctx")
    z, xh = dp // 2, lax.rem(dp, 2)
    xl, y, core = cx // 8, lax.rem(cx // 2, 4), lax.rem(cx, 2)
    chip, half = cx // 2, lax.rem(z, 2)
    other = 1 - core

    def at_y(step):
        return lax.rem(y + step, 4)

    sibling = (dp, chip * 2 + other)
    inner = (dp, (1 - xl) * 8 + y * 2 + core)
    outer = (z * 2 + 1 - xh, (1 - xl) * 8 + y * 2 + core)
    above = (lax.rem(z + 1, 4) * 2 + xh, cx)
    below = (lax.rem(z + 3, 4) * 2 + xh, cx)

    def peer(step):
        return lax.rem(chip + step, CHIPS)

    (hid_l, hid_s, hid_r, dst_s, dst_r, met_s, met_r) = (one.at[i] for i in range(7))
    (w_l, w_s, w_r, y_s, y_r, x_s, x_r, z_s, z_r, a_s, a_r, h_s, h_r, o_l, o_s, o_r, f_s, f_r) = (
        six.at[i] for i in range(18)
    )

    barrier = pltpu.get_barrier_semaphore()
    near = [sibling, outer, above, below] + [(dp, peer(r) * 2 + core) for r in range(1, CHIPS)]
    for device in near:
        pl.semaphore_signal(barrier, inc=1, device_id=device, device_id_type=MESH)
    pl.semaphore_wait(barrier, len(near))

    def remote(src, dst, s, r, device):
        return pltpu.make_async_remote_copy(
            src_ref=src, dst_ref=dst, send_sem=s, recv_sem=r, device_id=device, device_id_type=MESH
        )

    def drain(ref, sem):
        pltpu.make_async_copy(ref, ref, sem).wait()

    def columns(k, of):
        if k == 0:
            return wk.at[:, pl.ds(pl.multiple_of(of * WIDE, WIDE), WIDE)]
        if k == 1:
            return wv.at[:, pl.ds(pl.multiple_of(of * WIDE, WIDE), WIDE)]
        return wq.at[:, pl.ds(pl.multiple_of(of * 1024 + (k - 2) * WIDE, WIDE), WIDE)]

    mine = pl.ds(pl.multiple_of(core * 256, 256), 256)
    my_rows = pl.ds(pl.multiple_of(core * BLOCK, BLOCK), BLOCK)
    for k in range(CHUNKS):
        spot = w_all.at[k, 0, mine]
        remote(columns(k, other), spot, w_s.at[k], w_r.at[k], sibling).start()
        pltpu.make_async_copy(columns(k, core), spot, w_l.at[k]).start()
    dests[core] = jnp.broadcast_to(dest[...], (8, BLOCK))
    remote(dests.at[core], dests.at[core], dst_s, dst_r, sibling).start()

    def run(start, size):
        return pl.ds(pl.multiple_of(start, size), size)

    def part(k, shards):
        rows = run(z * 128, 128) if QUARTERS[k] else run(half * 256, 256)
        return w_all.at[k, shards, rows]

    def shape(k, n, rows):
        return w_all.at[k, pl.ds(0, n), pl.ds(0, rows)]

    def width(k):
        return 128 if QUARTERS[k] else 256

    def stage_y(k):
        own = w_all.at[k, 0, mine]
        drain(own, w_l.at[k])
        drain(own, w_r.at[k])
        for step in (1, 3, 2):
            remote(
                part(k, 0), part(k, 4 - step), y_s.at[k], y_r.at[k],
                (dp, xl * 8 + at_y(step) * 2 + core),
            ).start()
        remote(
            part(k, 0), part(k, 4), x_s.at[k], x_r.at[k], outer if QUARTERS[k] else inner
        ).start()

    def to_z(k, shards):
        for i, device in enumerate((below, above)):
            if QUARTERS[k]:
                spot = part(k, shards)
            else:
                spot = w_all.at[k, shards, run(half * 256 + i * 128, 128)]
            remote(spot, spot, z_s.at[k], z_r.at[k], device).start()

    def stage_x(k):
        drain(shape(k, 3, width(k)), y_r.at[k])
        remote(
            part(k, pl.ds(1, 3)), part(k, pl.ds(5, 3)), x_s.at[k], x_r.at[k], outer
        ).start()
        to_z(k, pl.ds(1, 3))

    def stage_z(k):
        drain(shape(k, 4, width(k)), x_r.at[k])
        to_z(k, pl.ds(4, 4))

    def stage_f(k):
        if QUARTERS[k]:
            drain(shape(k, 7, 256), z_r.at[k])
            spot = w_all.at[k, pl.ds(1, 7), run(lax.rem(z + 3, 4) * 128, 64)]
            remote(spot, spot, f_s.at[k], f_r.at[k], above).start()
            spot = w_all.at[k, pl.ds(1, 7), run(lax.rem(z + 1, 4) * 128 + 64, 64)]
            remote(spot, spot, f_s.at[k], f_r.at[k], below).start()

    def arrived(k):
        if QUARTERS[k]:
            drain(shape(k, 7, 128), f_r.at[k])
        else:
            drain(shape(k, 7, 256), z_r.at[k])

    def at_step(i, late, stage):
        for k in range(max(late, 0), CHUNKS):
            pl.when(i == k - late)(lambda k=k: stage(k))

    def project(k):
        at_step(k, 0, arrived)

        def rows(m, _):
            at = pl.ds(pl.multiple_of(m * 512, 512), 512)
            qkv[at, :] = jnp.dot(
                x_all[at, :], w_all[k].reshape(CHIPS * 512, WIDE), preferred_element_type=F32
            ).astype(BF16)
            return 0

        lax.fori_loop(0, 2, rows, 0)

        def send(r, _):
            j = peer(r)
            snd[k, j] = jnp.dot(
                pack[pl.ds(pl.multiple_of(j * SLOTS, SLOTS), SLOTS), :], qkv[...],
                preferred_element_type=F32,
            ).astype(BF16)
            remote(
                snd.at[k, j], rcv.at[k, chip], a_s.at[k], a_r.at[k], (dp, j * 2 + core)
            ).start()
            return 0

        lax.fori_loop(1, CHIPS, send, 0)
        rcv[k, chip] = jnp.dot(
            pack[pl.ds(pl.multiple_of(chip * SLOTS, SLOTS), SLOTS), :], qkv[...],
            preferred_element_type=F32,
        ).astype(BF16)

    def placed(k, t):
        got = rcv[k, :, pl.ds(pl.multiple_of(t * 128, 128), 128), :].reshape(CHIPS * 128, WIDE)
        return jnp.dot(unpack[t], got, preferred_element_type=F32)

    def turned(v, t):
        at = pl.ds(pl.multiple_of(t * BLOCK, BLOCK), BLOCK)
        return (v * cos[at, :] + pltpu.roll(v, 64, 1) * sin[at, :]).astype(BF16)

    following = (dp, peer(1) * 2 + core)

    def halo(ref, i):
        remote(
            ref.at[:, pl.ds(1024, 512)], ref.at[:, pl.ds(0, 512)], h_s.at[i], h_r.at[i], following
        ).start()

    def receive(k):
        drain(rcv.at[k, pl.ds(0, 7)], a_r.at[k])

        def block(t, _):
            v = placed(k, t)
            for h in range(2):
                head = v[:, h * HEAD : (h + 1) * HEAD]

                @pl.when(k == 0)
                def _():
                    keys[h, pl.ds(pl.multiple_of(512 + t * 512, 512), 512), :] = turned(head, t)

                @pl.when(k == 1)
                def _():
                    vals[h, pl.ds(pl.multiple_of(512 + t * 512, 512), 512), :] = head.astype(BF16)

                @pl.when(k >= 2)
                def _():
                    qs[h, pl.ds(pl.multiple_of(t * 512, 512), 512), :] = turned(head, t)

            return 0

        lax.fori_loop(0, 2, block, 0)

        @pl.when(k == 0)
        def _():
            halo(keys, 0)

        @pl.when(k == 1)
        def _():
            halo(vals, 1)

        @pl.when(k == 2)
        def _():
            drain(keys.at[:, pl.ds(0, 512)], h_r.at[0])
            drain(vals.at[:, pl.ds(0, 512)], h_r.at[1])

        @pl.when(k >= 2)
        def _():
            attend(k - 2)

    def attend(c):
        g = c // 2

        def tile(n, _):
            i = lax.rem(n + other * 4, 8)
            at = pl.multiple_of(i * 128, 128)
            q = qs[:, pl.ds(at, 128), :].reshape(256, HEAD)
            s = lax.dot_general(
                q, keys[g, pl.ds(at, WINDOW), :], (((1,), (1,)), ((), ())),
                preferred_element_type=F32,
            )
            s = s.reshape(2, 128, WINDOW) * SCORE + bias[i][None]
            s = s.reshape(256, WINDOW)
            e = jnp.exp2(s - jnp.max(s, axis=1, keepdims=True))
            total = jnp.sum(e, axis=1, keepdims=True)
            o = jnp.dot(e.astype(BF16), vals[g, pl.ds(at, WINDOW), :], preferred_element_type=F32)
            o = (o / total).astype(BF16)
            to = pl.ds(pl.multiple_of(lax.rem(i, 4) * 128, 128), 128)
            outs[i // 4, c, to, pl.ds(0, HEAD)] = o[:128]
            outs[i // 4, c, to, pl.ds(HEAD, HEAD)] = o[128:]
            return 0

        lax.fori_loop(0, 4, tile, 0)
        spot = out.at[:, pl.ds(pl.multiple_of(core * 1024 + c * WIDE, WIDE), WIDE)]
        remote(outs.at[other, c], spot, o_s.at[c], o_r.at[c], sibling).start()
        lax.fori_loop(4, 8, tile, 0)
        pltpu.make_async_copy(outs.at[core, c], spot, o_l.at[c]).start()

    stage_y(0)
    stage_y(1)
    stage_y(2)
    stage_y(3)
    for r in range(CHIPS):
        shard = (xl if r < 4 else 1 - xl) * 4 + at_y(r % 4)
        src = hid.at[:, run(shard * 512, 512)]
        spot = x_all.at[my_rows, pl.ds(r * 512, 512)]
        remote(src, spot, hid_s, hid_r, sibling).start()
        pltpu.make_async_copy(src, spot, hid_l).start()

    drain(dests.at[core], dst_r)
    tri = (
        lax.broadcasted_iota(jnp.int32, (BLOCK, BLOCK), 0)
        <= lax.broadcasted_iota(jnp.int32, (BLOCK, BLOCK), 1)
    ).astype(BF16)
    targets = jnp.zeros((8, CHIPS * SLOTS), F32)
    for b in range(2):
        d = dests[b][:1]
        owner = lax.shift_right_logical(d, 9)
        hits = lax.broadcasted_iota(jnp.int32, (16, BLOCK), 0) == owner
        counts = jnp.dot(hits.astype(BF16), tri, preferred_element_type=F32)
        rank = jnp.sum(jnp.where(hits, counts, 0.0), axis=0, keepdims=True) - 1.0
        slot = (owner * 2 + b) * 64 + rank.astype(jnp.int32)

        def fill(m, _):
            at = pl.multiple_of(m * 256, 256)
            pack[pl.ds(at, 256), pl.ds(b * BLOCK, BLOCK)] = (
                lax.broadcasted_iota(jnp.int32, (256, BLOCK), 0) + at == slot
            ).astype(BF16)
            return 0

        lax.fori_loop(0, 8, fill, 0)
        target = jnp.bitwise_and(d, 511) + 1
        row = lax.broadcasted_iota(jnp.int32, (8, BLOCK), 0)
        digits = jnp.where(
            row == 0,
            lax.shift_right_logical(target, 5),
            jnp.where(row == 1, jnp.bitwise_and(target, 31), 0),
        )
        targets = targets + lax.dot_general(
            digits.astype(F32).astype(BF16), pack[:, b * BLOCK : (b + 1) * BLOCK],
            (((1,), (1,)), ((), ())), preferred_element_type=F32,
        )
    targets = targets[:1] * 32.0 + targets[1:2]
    for j in range(CHIPS):
        for t in range(2):
            at = (j * 2 + t) * 128
            meta_s[j, t : t + 1, :] = targets[:, at : at + 128]
        meta_s[j, 2:8, :] = jnp.zeros((6, 128), F32)
    for r in range(1, CHIPS):
        j = peer(r)
        remote(meta_s.at[j], meta_r.at[chip], met_s, met_r, (dp, j * 2 + core)).start()
    meta_r[chip] = meta_s[chip]

    stage_x(0)
    stage_y(4)

    def mask(i, _):
        def doc(at):
            line = docs[pl.ds(jnp.maximum(at, 0), 1), :].astype(F32)
            return jnp.where(at >= 0, line, -1.0)

        own = jnp.transpose(jnp.broadcast_to(doc(chip * 8 + i), (128, 128)))
        row = lax.broadcasted_iota(jnp.int32, (128, 128), 0)
        for j in range(5):
            col = lax.broadcasted_iota(jnp.int32, (128, 128), 1) + j * 128
            seen = (col > row) & (col <= row + 512) & (own == doc(chip * 8 - 4 + i + j))
            bias[i, :, j * 128 : (j + 1) * 128] = jnp.where(seen, 0.0, -1e30)
        return 0

    lax.fori_loop(0, 8, mask, 0)

    stage_x(1)
    stage_y(5)
    stage_z(0)

    cc, cs = table[pl.ds(chip, 1), :], table[pl.ds(8 + chip, 1), :]
    turn[0] = table[16:48, :] * cc - table[48:80, :] * cs
    turn[1] = table[48:80, :] * cc + table[16:48, :] * cs
    sign = jnp.where(lax.broadcasted_iota(jnp.int32, (1, HEAD), 1) < 64, -1.0, 1.0)

    def rotary(i, _):
        at = run(i * 32, 32)
        ca, sa = turn[0, pl.ds(i, 1), :], turn[1, pl.ds(i, 1), :]
        cos[at, :] = table[80:112, :] * ca - table[112:144, :] * sa
        sin[at, :] = (table[112:144, :] * ca + table[80:112, :] * sa) * sign
        return 0

    lax.fori_loop(0, 32, rotary, 0)

    stage_x(2)
    stage_z(1)

    drain(meta_r.at[pl.ds(0, 7)], met_r)
    place = lax.broadcasted_iota(jnp.int32, (BLOCK, 128), 0).astype(F32) + 1.0
    for t in range(2):
        for i in range(CHIPS):
            unpack[t, :, i * 128 : (i + 1) * 128] = (place == meta_r[i, t : t + 1, :]).astype(BF16)

    drain(x_all.at[my_rows], hid_l)
    drain(x_all.at[my_rows], hid_r)

    def step(i, _):
        @pl.when(i < CHUNKS)
        def _():
            project(i)

        at_step(i, 3, stage_x)
        at_step(i, 2, stage_z)
        at_step(i, 1, stage_f)

        @pl.when(i >= 1)
        def _():
            receive(i - 1)

        return 0

    lax.fori_loop(0, CHUNKS + 1, step, 0)

    for c in range(4):
        spot = out.at[:, pl.ds(c * WIDE, WIDE)]
        drain(spot, o_l.at[c])
        drain(spot, o_r.at[c])
        drain(outs.at[0, c], o_s.at[c])
    for k in range(CHUNKS):
        drain(shape(k, 1, 256), w_s.at[k])
        drain(shape(k, 3, width(k)), y_s.at[k])
        drain(shape(k, 4, width(k)), x_s.at[k])
        drain(shape(k, 7, 256), z_s.at[k])
        if QUARTERS[k]:
            drain(shape(k, 7, 128), f_s.at[k])
        drain(snd.at[k, pl.ds(0, 7)], a_s.at[k])
    drain(keys.at[:, pl.ds(0, 512)], h_s.at[0])
    drain(vals.at[:, pl.ds(0, 512)], h_s.at[1])
    drain(x_all.at[my_rows], hid_s)
    drain(dests.at[core], dst_s)
    drain(meta_s.at[pl.ds(0, 7)], met_s)


def on_device(hidden, dest, doc_ids, w_query, key_weight, value_weight):
    anywhere = pl.BlockSpec(memory_space=pl.ANY)
    local = pl.BlockSpec(memory_space=pltpu.VMEM)
    return pl.pallas_call(
        kernel,
        out_shape=pltpu.VMEM((BLOCK, 2048), BF16),
        in_specs=[anywhere, local, local, local, anywhere, anywhere, anywhere],
        out_specs=local,
        scratch_shapes=[
            pltpu.VMEM((1024, HEAD), F32),
            pltpu.VMEM((1024, HEAD), F32),
            pltpu.VMEM((2, 32, HEAD), F32),
            pltpu.VMEM((1024, 4096), BF16),
            pltpu.VMEM((CHUNKS, CHIPS, 512, WIDE), BF16),
            pltpu.VMEM((2, 8, BLOCK), jnp.int32),
            pltpu.VMEM((CHIPS * SLOTS, 1024), BF16),
            pltpu.VMEM((2, BLOCK, 1024), BF16),
            pltpu.VMEM((CHIPS, 8, 128), F32),
            pltpu.VMEM((CHIPS, 8, 128), F32),
            pltpu.VMEM((1024, WIDE), BF16),
            pltpu.VMEM((CHUNKS, CHIPS, SLOTS, WIDE), BF16),
            pltpu.VMEM((CHUNKS, CHIPS, SLOTS, WIDE), BF16),
            pltpu.VMEM((2, 1536, HEAD), BF16),
            pltpu.VMEM((2, 1536, HEAD), BF16),
            pltpu.VMEM((2, 1024, HEAD), BF16),
            pltpu.VMEM((2, 4, BLOCK, WIDE), BF16),
            pltpu.VMEM((8, 128, WINDOW), F32),
            pltpu.SemaphoreType.DMA((7,)),
            pltpu.SemaphoreType.DMA((18, CHUNKS)),
        ],
        compiler_params=pltpu.CompilerParams(
            collective_id=0, has_side_effects=True, vmem_limit_bytes=60 * 2**20
        ),
    )(
        hidden, dest.reshape(1, BLOCK), doc_ids.reshape(64, 128), jnp.asarray(angles()),
        w_query, key_weight, value_weight,
    )


def solution(mesh):
    placed = (
        P(("dp", "ctx"), None),
        P(("dp", "ctx")),
        P("dp"),
        P("ctx", None),
        P("ctx", None),
        P("ctx", None),
    )
    return jax.shard_map(
        on_device, mesh=mesh, in_specs=placed, out_specs=P(("dp", "ctx"), None), check_vma=False
    )
```

```python
import jax
import jax.numpy as jnp
import numpy as np
from jax import lax
from jax.experimental import pallas as pl
from jax.experimental.pallas import tpu as pltpu
from jax.sharding import PartitionSpec as P

HEAD = 128
BLOCK = 512
CHIPS = 8
CHUNKS = 6
WIDE = 256
SLOTS = 256
WINDOW = 640
MESH = pl.DeviceIdType.MESH
rope_base = 500000.0 * 16.0 ** (128.0 / 126.0)
SCORE = HEAD**-0.5 * 1.4426950408889634
F32, BF16 = jnp.float32, jnp.bfloat16
QUARTERS = (False, False, False, False, True, True)


def angles():
    inverse = rope_base ** (-2.0 * np.arange(64) / HEAD)
    steps = [np.arange(8) * 1024, np.arange(32) * 32, np.arange(32)]
    parts = []
    for at in steps:
        angle = at[:, None] * inverse[None, :]
        parts += [np.tile(np.cos(angle), (1, 2)), np.tile(np.sin(angle), (1, 2))]
    return np.concatenate(parts).astype(np.float32)


def kernel(
    hid, dest, docs, table, wq, wk, wv, out,
    cos, sin, turn, x_all, w_all, dests, pack, unpack, meta_s, meta_r, qkv, snd, rcv, keys, vals, qs, outs, bias,
    one, six,
):
    dp, cx = lax.axis_index("dp"), lax.axis_index("ctx")
    z, xh = dp // 2, lax.rem(dp, 2)
    xl, y, core = cx // 8, lax.rem(cx // 2, 4), lax.rem(cx, 2)
    chip, half = cx // 2, lax.rem(z, 2)
    other = 1 - core

    def at_y(step):
        return lax.rem(y + step, 4)

    sibling = (dp, chip * 2 + other)
    inner = (dp, (1 - xl) * 8 + y * 2 + core)
    outer = (z * 2 + 1 - xh, (1 - xl) * 8 + y * 2 + core)
    above = (lax.rem(z + 1, 4) * 2 + xh, cx)
    below = (lax.rem(z + 3, 4) * 2 + xh, cx)

    def peer(step):
        return lax.rem(chip + step, CHIPS)

    (hid_l, hid_s, hid_r, dst_s, dst_r, met_s, met_r) = (one.at[i] for i in range(7))
    (w_l, w_s, w_r, y_s, y_r, x_s, x_r, z_s, z_r, a_s, a_r, h_s, h_r, o_l, o_s, o_r, f_s, f_r) = (
        six.at[i] for i in range(18)
    )

    barrier = pltpu.get_barrier_semaphore()
    near = [sibling, outer, above, below] + [(dp, peer(r) * 2 + core) for r in range(1, CHIPS)]
    for device in near:
        pl.semaphore_signal(barrier, inc=1, device_id=device, device_id_type=MESH)
    pl.semaphore_wait(barrier, len(near))

    def remote(src, dst, s, r, device):
        return pltpu.make_async_remote_copy(
            src_ref=src, dst_ref=dst, send_sem=s, recv_sem=r, device_id=device, device_id_type=MESH
        )

    def drain(ref, sem):
        pltpu.make_async_copy(ref, ref, sem).wait()

    def columns(k, of):
        if k == 0:
            return wk.at[:, pl.ds(pl.multiple_of(of * WIDE, WIDE), WIDE)]
        if k == 1:
            return wv.at[:, pl.ds(pl.multiple_of(of * WIDE, WIDE), WIDE)]
        return wq.at[:, pl.ds(pl.multiple_of(of * 1024 + (k - 2) * WIDE, WIDE), WIDE)]

    mine = pl.ds(pl.multiple_of(core * 256, 256), 256)
    my_rows = pl.ds(pl.multiple_of(core * BLOCK, BLOCK), BLOCK)
    def shard_in(k):
        spot = w_all.at[k, 0, mine]
        remote(columns(k, other), spot, w_s.at[k], w_r.at[k], sibling).start()
        pltpu.make_async_copy(columns(k, core), spot, w_l.at[k]).start()

    shard_in(0)
    dests[core] = jnp.broadcast_to(dest[...], (8, BLOCK))
    remote(dests.at[core], dests.at[core], dst_s, dst_r, sibling).start()

    def run(start, size):
        return pl.ds(pl.multiple_of(start, size), size)

    def part(k, shards):
        rows = run(z * 128, 128) if QUARTERS[k] else run(half * 256, 256)
        return w_all.at[k, shards, rows]

    def shape(k, n, rows):
        return w_all.at[k, pl.ds(0, n), pl.ds(0, rows)]

    def width(k):
        return 128 if QUARTERS[k] else 256

    def stage_y(k):
        own = w_all.at[k, 0, mine]
        drain(own, w_l.at[k])
        drain(own, w_r.at[k])
        for step in (1, 3, 2):
            remote(
                part(k, 0), part(k, 4 - step), y_s.at[k], y_r.at[k],
                (dp, xl * 8 + at_y(step) * 2 + core),
            ).start()
        remote(
            part(k, 0), part(k, 4), x_s.at[k], x_r.at[k], outer if QUARTERS[k] else inner
        ).start()

    def to_z(k, shards):
        for i, device in enumerate((below, above)):
            if QUARTERS[k]:
                spot = part(k, shards)
            else:
                spot = w_all.at[k, shards, run(half * 256 + i * 128, 128)]
            remote(spot, spot, z_s.at[k], z_r.at[k], device).start()

    def stage_x(k):
        drain(shape(k, 3, width(k)), y_r.at[k])
        moves = ((1, 1, inner), (2, 2, outer)) if k in (0,) else ((1, 3, outer),)
        for first, count, device in moves:
            remote(
                part(k, pl.ds(first, count)), part(k, pl.ds(4 + first, count)),
                x_s.at[k], x_r.at[k], device,
            ).start()
        to_z(k, pl.ds(1, 3))

    def stage_z(k):
        drain(shape(k, 4, width(k)), x_r.at[k])
        to_z(k, pl.ds(4, 4))

    def stage_f(k):
        if QUARTERS[k]:
            drain(shape(k, 7, 256), z_r.at[k])
            spot = w_all.at[k, pl.ds(1, 7), run(lax.rem(z + 3, 4) * 128, 64)]
            remote(spot, spot, f_s.at[k], f_r.at[k], above).start()
            spot = w_all.at[k, pl.ds(1, 7), run(lax.rem(z + 1, 4) * 128 + 64, 64)]
            remote(spot, spot, f_s.at[k], f_r.at[k], below).start()

    def arrived(k):
        if QUARTERS[k]:
            drain(shape(k, 7, 128), f_r.at[k])
        else:
            drain(shape(k, 7, 256), z_r.at[k])

    def at_step(i, late, stage):
        for k in range(max(late, 0), CHUNKS):
            pl.when(i == k - late)(lambda k=k: stage(k))

    def project(k):
        at_step(k, 0, arrived)

        def rows(m, _):
            at = pl.ds(pl.multiple_of(m * 512, 512), 512)
            qkv[at, :] = jnp.dot(
                x_all[at, :], w_all[k].reshape(CHIPS * 512, WIDE), preferred_element_type=F32
            ).astype(BF16)
            return 0

        lax.fori_loop(0, 2, rows, 0)

        def send(r, _):
            j = peer(r)
            snd[k, j] = jnp.dot(
                pack[pl.ds(pl.multiple_of(j * SLOTS, SLOTS), SLOTS), :], qkv[...],
                preferred_element_type=F32,
            ).astype(BF16)
            remote(
                snd.at[k, j], rcv.at[k, chip], a_s.at[k], a_r.at[k], (dp, j * 2 + core)
            ).start()
            return 0

        lax.fori_loop(1, CHIPS, send, 0)
        rcv[k, chip] = jnp.dot(
            pack[pl.ds(pl.multiple_of(chip * SLOTS, SLOTS), SLOTS), :], qkv[...],
            preferred_element_type=F32,
        ).astype(BF16)

    def placed(k, t):
        got = rcv[k, :, pl.ds(pl.multiple_of(t * 128, 128), 128), :].reshape(CHIPS * 128, WIDE)
        return jnp.dot(unpack[t], got, preferred_element_type=F32)

    def turned(v, t):
        at = pl.ds(pl.multiple_of(t * BLOCK, BLOCK), BLOCK)
        return (v * cos[at, :] + pltpu.roll(v, 64, 1) * sin[at, :]).astype(BF16)

    following = (dp, peer(1) * 2 + core)

    def halo(ref, i):
        remote(
            ref.at[:, pl.ds(1024, 512)], ref.at[:, pl.ds(0, 512)], h_s.at[i], h_r.at[i], following
        ).start()

    def receive(k):
        drain(rcv.at[k, pl.ds(0, 7)], a_r.at[k])

        def block(t, _):
            v = placed(k, t)
            for h in range(2):
                head = v[:, h * HEAD : (h + 1) * HEAD]

                @pl.when(k == 0)
                def _():
                    keys[h, pl.ds(pl.multiple_of(512 + t * 512, 512), 512), :] = turned(head, t)

                @pl.when(k == 1)
                def _():
                    vals[h, pl.ds(pl.multiple_of(512 + t * 512, 512), 512), :] = head.astype(BF16)

                @pl.when(k >= 2)
                def _():
                    qs[h, pl.ds(pl.multiple_of(t * 512, 512), 512), :] = turned(head, t)

            return 0

        lax.fori_loop(0, 2, block, 0)

        @pl.when(k == 0)
        def _():
            halo(keys, 0)

        @pl.when(k == 1)
        def _():
            halo(vals, 1)

        @pl.when(k == 2)
        def _():
            drain(keys.at[:, pl.ds(0, 512)], h_r.at[0])
            drain(vals.at[:, pl.ds(0, 512)], h_r.at[1])

        @pl.when(k >= 2)
        def _():
            attend(k - 2)

    def attend(c):
        g = c // 2

        def tile(n, _):
            i = lax.rem(n + other * 4, 8)
            at = pl.multiple_of(i * 128, 128)
            q = qs[:, pl.ds(at, 128), :].reshape(256, HEAD)
            s = lax.dot_general(
                q, keys[g, pl.ds(at, WINDOW), :], (((1,), (1,)), ((), ())),
                preferred_element_type=F32,
            )
            s = s.reshape(2, 128, WINDOW) * SCORE + bias[i][None]
            s = s.reshape(256, WINDOW)
            e = jnp.exp2(s - jnp.max(s, axis=1, keepdims=True))
            total = jnp.sum(e, axis=1, keepdims=True)
            o = jnp.dot(e.astype(BF16), vals[g, pl.ds(at, WINDOW), :], preferred_element_type=F32)
            o = (o / total).astype(BF16)
            to = pl.ds(pl.multiple_of(lax.rem(i, 4) * 128, 128), 128)
            outs[i // 4, c, to, pl.ds(0, HEAD)] = o[:128]
            outs[i // 4, c, to, pl.ds(HEAD, HEAD)] = o[128:]
            return 0

        lax.fori_loop(0, 4, tile, 0, unroll=4)
        spot = out.at[:, pl.ds(pl.multiple_of(core * 1024 + c * WIDE, WIDE), WIDE)]
        remote(outs.at[other, c], spot, o_s.at[c], o_r.at[c], sibling).start()
        lax.fori_loop(4, 8, tile, 0, unroll=4)
        pltpu.make_async_copy(outs.at[core, c], spot, o_l.at[c]).start()

    stage_y(0)
    for k in range(1, CHUNKS):
        shard_in(k)
    stage_y(1)
    stage_y(2)
    stage_y(3)
    drain(dests.at[core], dst_r)
    tri = (
        lax.broadcasted_iota(jnp.int32, (BLOCK, BLOCK), 0)
        <= lax.broadcasted_iota(jnp.int32, (BLOCK, BLOCK), 1)
    ).astype(BF16)
    targets = jnp.zeros((8, CHIPS * SLOTS), F32)
    for b in range(2):
        d = dests[b][:1]
        owner = lax.shift_right_logical(d, 9)
        hits = lax.broadcasted_iota(jnp.int32, (16, BLOCK), 0) == owner
        counts = jnp.dot(hits.astype(BF16), tri, preferred_element_type=F32)
        rank = jnp.sum(jnp.where(hits, counts, 0.0), axis=0, keepdims=True) - 1.0
        slot = (owner * 2 + b) * 64 + rank.astype(jnp.int32)

        def fill(m, _):
            at = pl.multiple_of(m * 256, 256)
            pack[pl.ds(at, 256), pl.ds(b * BLOCK, BLOCK)] = (
                lax.broadcasted_iota(jnp.int32, (256, BLOCK), 0) + at == slot
            ).astype(BF16)
            return 0

        lax.fori_loop(0, 8, fill, 0)
        target = jnp.bitwise_and(d, 511) + 1
        row = lax.broadcasted_iota(jnp.int32, (8, BLOCK), 0)
        digits = jnp.where(
            row == 0,
            lax.shift_right_logical(target, 5),
            jnp.where(row == 1, jnp.bitwise_and(target, 31), 0),
        )
        targets = targets + lax.dot_general(
            digits.astype(F32).astype(BF16), pack[:, b * BLOCK : (b + 1) * BLOCK],
            (((1,), (1,)), ((), ())), preferred_element_type=F32,
        )
    targets = targets[:1] * 32.0 + targets[1:2]
    for j in range(CHIPS):
        for t in range(2):
            at = (j * 2 + t) * 128
            meta_s[j, t : t + 1, :] = targets[:, at : at + 128]
        meta_s[j, 2:8, :] = jnp.zeros((6, 128), F32)
    for r in range(1, CHIPS):
        j = peer(r)
        remote(meta_s.at[j], meta_r.at[chip], met_s, met_r, (dp, j * 2 + core)).start()
    meta_r[chip] = meta_s[chip]

    stage_x(0)
    stage_y(4)

    for r in range(CHIPS):
        shard = (xl if r < 4 else 1 - xl) * 4 + at_y(r % 4)
        src = hid.at[:, run(shard * 512, 512)]
        spot = x_all.at[my_rows, pl.ds(r * 512, 512)]
        remote(src, spot, hid_s, hid_r, sibling).start()
        pltpu.make_async_copy(src, spot, hid_l).start()

    def mask(i, _):
        def doc(at):
            line = docs[pl.ds(jnp.maximum(at, 0), 1), :].astype(F32)
            return jnp.where(at >= 0, line, -1.0)

        own = jnp.transpose(jnp.broadcast_to(doc(chip * 8 + i), (128, 128)))
        row = lax.broadcasted_iota(jnp.int32, (128, 128), 0)
        for j in range(5):
            col = lax.broadcasted_iota(jnp.int32, (128, 128), 1) + j * 128
            seen = (col > row) & (col <= row + 512) & (own == doc(chip * 8 - 4 + i + j))
            bias[i, :, j * 128 : (j + 1) * 128] = jnp.where(seen, 0.0, -1e30)
        return 0

    lax.fori_loop(0, 8, mask, 0)

    stage_x(1)
    stage_y(5)
    stage_z(0)

    cc, cs = table[pl.ds(chip, 1), :], table[pl.ds(8 + chip, 1), :]
    turn[0] = table[16:48, :] * cc - table[48:80, :] * cs
    turn[1] = table[48:80, :] * cc + table[16:48, :] * cs
    sign = jnp.where(lax.broadcasted_iota(jnp.int32, (1, HEAD), 1) < 64, -1.0, 1.0)

    def rotary(i, _):
        at = run(i * 32, 32)
        ca, sa = turn[0, pl.ds(i, 1), :], turn[1, pl.ds(i, 1), :]
        cos[at, :] = table[80:112, :] * ca - table[112:144, :] * sa
        sin[at, :] = (table[112:144, :] * ca + table[80:112, :] * sa) * sign
        return 0

    lax.fori_loop(0, 32, rotary, 0)

    stage_x(2)
    stage_z(1)

    drain(meta_r.at[pl.ds(0, 7)], met_r)
    place = lax.broadcasted_iota(jnp.int32, (BLOCK, 128), 0).astype(F32) + 1.0
    for t in range(2):
        for i in range(CHIPS):
            unpack[t, :, i * 128 : (i + 1) * 128] = (place == meta_r[i, t : t + 1, :]).astype(BF16)

    drain(x_all.at[my_rows], hid_l)
    drain(x_all.at[my_rows], hid_r)

    def step(i, _):
        @pl.when(i < CHUNKS)
        def _():
            project(i)

        at_step(i, 3, stage_x)
        at_step(i, 2, stage_z)
        at_step(i, 1, stage_f)

        @pl.when(i >= 1)
        def _():
            receive(i - 1)

        return 0

    lax.fori_loop(0, CHUNKS + 1, step, 0)

    for c in range(4):
        spot = out.at[:, pl.ds(c * WIDE, WIDE)]
        drain(spot, o_l.at[c])
        drain(spot, o_r.at[c])
        drain(outs.at[0, c], o_s.at[c])
    for k in range(CHUNKS):
        drain(shape(k, 1, 256), w_s.at[k])
        drain(shape(k, 3, width(k)), y_s.at[k])
        drain(shape(k, 4, width(k)), x_s.at[k])
        drain(shape(k, 7, 256), z_s.at[k])
        if QUARTERS[k]:
            drain(shape(k, 7, 128), f_s.at[k])
        drain(snd.at[k, pl.ds(0, 7)], a_s.at[k])
    drain(keys.at[:, pl.ds(0, 512)], h_s.at[0])
    drain(vals.at[:, pl.ds(0, 512)], h_s.at[1])
    drain(x_all.at[my_rows], hid_s)
    drain(dests.at[core], dst_s)
    drain(meta_s.at[pl.ds(0, 7)], met_s)


def on_device(hidden, dest, doc_ids, w_query, key_weight, value_weight):
    anywhere = pl.BlockSpec(memory_space=pl.ANY)
    local = pl.BlockSpec(memory_space=pltpu.VMEM)
    return pl.pallas_call(
        kernel,
        out_shape=pltpu.VMEM((BLOCK, 2048), BF16),
        in_specs=[anywhere, local, local, local, anywhere, anywhere, anywhere],
        out_specs=local,
        scratch_shapes=[
            pltpu.VMEM((1024, HEAD), F32),
            pltpu.VMEM((1024, HEAD), F32),
            pltpu.VMEM((2, 32, HEAD), F32),
            pltpu.VMEM((1024, 4096), BF16),
            pltpu.VMEM((CHUNKS, CHIPS, 512, WIDE), BF16),
            pltpu.VMEM((2, 8, BLOCK), jnp.int32),
            pltpu.VMEM((CHIPS * SLOTS, 1024), BF16),
            pltpu.VMEM((2, BLOCK, 1024), BF16),
            pltpu.VMEM((CHIPS, 8, 128), F32),
            pltpu.VMEM((CHIPS, 8, 128), F32),
            pltpu.VMEM((1024, WIDE), BF16),
            pltpu.VMEM((CHUNKS, CHIPS, SLOTS, WIDE), BF16),
            pltpu.VMEM((CHUNKS, CHIPS, SLOTS, WIDE), BF16),
            pltpu.VMEM((2, 1536, HEAD), BF16),
            pltpu.VMEM((2, 1536, HEAD), BF16),
            pltpu.VMEM((2, 1024, HEAD), BF16),
            pltpu.VMEM((2, 4, BLOCK, WIDE), BF16),
            pltpu.VMEM((8, 128, WINDOW), F32),
            pltpu.SemaphoreType.DMA((7,)),
            pltpu.SemaphoreType.DMA((18, CHUNKS)),
        ],
        compiler_params=pltpu.CompilerParams(
            collective_id=0, has_side_effects=True, vmem_limit_bytes=60 * 2**20
        ),
    )(
        hidden, dest.reshape(1, BLOCK), doc_ids.reshape(64, 128), jnp.asarray(angles()),
        w_query, key_weight, value_weight,
    )


def solution(mesh):
    placed = (
        P(("dp", "ctx"), None),
        P(("dp", "ctx")),
        P("dp"),
        P("ctx", None),
        P("ctx", None),
        P("ctx", None),
    )
    return jax.shard_map(
        on_device, mesh=mesh, in_specs=placed, out_specs=P(("dp", "ctx"), None), check_vma=False
    )
```

```python
import jax
import jax.numpy as jnp
import numpy as np
from jax import lax
from jax.experimental import pallas as pl
from jax.experimental.pallas import tpu as pltpu
from jax.sharding import PartitionSpec as P

HEAD = 128
BLOCK = 512
CHIPS = 8
CHUNKS = 6
WIDE = 256
SLOTS = 256
WINDOW = 640
MESH = pl.DeviceIdType.MESH
rope_base = 500000.0 * 16.0 ** (128.0 / 126.0)
SCORE = HEAD**-0.5 * 1.4426950408889634
F32, BF16 = jnp.float32, jnp.bfloat16
BOTH = (0, 5)
QUARTERS = (False, False, False, False, True, True)


def angles():
    inverse = rope_base ** (-2.0 * np.arange(64) / HEAD)
    steps = [np.arange(8) * 1024, np.arange(32) * 32, np.arange(32)]
    parts = []
    for at in steps:
        angle = at[:, None] * inverse[None, :]
        parts += [np.tile(np.cos(angle), (1, 2)), np.tile(np.sin(angle), (1, 2))]
    return np.concatenate(parts).astype(np.float32)


def kernel(
    hid, dest, docs, table, wq, wk, wv, out,
    cos, sin, turn, x_all, w_all, dests, pack, unpack, meta_s, meta_r, qkv, snd, rcv, keys, vals, qs, outs, bias,
    one, six,
):
    dp, cx = lax.axis_index("dp"), lax.axis_index("ctx")
    z, xh = dp // 2, lax.rem(dp, 2)
    xl, y, core = cx // 8, lax.rem(cx // 2, 4), lax.rem(cx, 2)
    chip, half = cx // 2, lax.rem(z, 2)
    other = 1 - core

    def at_y(step):
        return lax.rem(y + step, 4)

    sibling = (dp, chip * 2 + other)
    inner = (dp, (1 - xl) * 8 + y * 2 + core)
    outer = (z * 2 + 1 - xh, (1 - xl) * 8 + y * 2 + core)
    above = (lax.rem(z + 1, 4) * 2 + xh, cx)
    below = (lax.rem(z + 3, 4) * 2 + xh, cx)

    def peer(step):
        return lax.rem(chip + step, CHIPS)

    (hid_l, hid_s, hid_r, dst_s, dst_r, met_s, met_r) = (one.at[i] for i in range(7))
    (w_l, w_s, w_r, y_s, y_r, x_s, x_r, z_s, z_r, a_s, a_r, h_s, h_r, o_l, o_s, o_r, f_s, f_r) = (
        six.at[i] for i in range(18)
    )

    barrier = pltpu.get_barrier_semaphore()
    near = [sibling, outer, above, below] + [(dp, peer(r) * 2 + core) for r in range(1, CHIPS)]
    for device in near:
        pl.semaphore_signal(barrier, inc=1, device_id=device, device_id_type=MESH)
    pl.semaphore_wait(barrier, len(near))

    def remote(src, dst, s, r, device):
        return pltpu.make_async_remote_copy(
            src_ref=src, dst_ref=dst, send_sem=s, recv_sem=r, device_id=device, device_id_type=MESH
        )

    def drain(ref, sem):
        pltpu.make_async_copy(ref, ref, sem).wait()

    def columns(k, of):
        if k == 0:
            return wk.at[:, pl.ds(pl.multiple_of(of * WIDE, WIDE), WIDE)]
        if k == 1:
            return wv.at[:, pl.ds(pl.multiple_of(of * WIDE, WIDE), WIDE)]
        return wq.at[:, pl.ds(pl.multiple_of(of * 1024 + (k - 2) * WIDE, WIDE), WIDE)]

    mine = pl.ds(pl.multiple_of(core * 256, 256), 256)
    my_rows = pl.ds(pl.multiple_of(core * BLOCK, BLOCK), BLOCK)
    def shard_in(k):
        spot = w_all.at[k, 0, mine]
        remote(columns(k, other), spot, w_s.at[k], w_r.at[k], sibling).start()
        pltpu.make_async_copy(columns(k, core), spot, w_l.at[k]).start()

    shard_in(0)
    dests[core] = jnp.broadcast_to(dest[...], (8, BLOCK))
    remote(dests.at[core], dests.at[core], dst_s, dst_r, sibling).start()

    def run(start, size):
        return pl.ds(pl.multiple_of(start, size), size)

    def part(k, shards):
        rows = run(z * 128, 128) if QUARTERS[k] else run(half * 256, 256)
        return w_all.at[k, shards, rows]

    def shape(k, n, rows):
        return w_all.at[k, pl.ds(0, n), pl.ds(0, rows)]

    def width(k):
        return 128 if QUARTERS[k] else 256

    def stage_y(k):
        own = w_all.at[k, 0, mine]
        drain(own, w_l.at[k])
        drain(own, w_r.at[k])
        for step in (1, 3, 2):
            remote(
                part(k, 0), part(k, 4 - step), y_s.at[k], y_r.at[k],
                (dp, xl * 8 + at_y(step) * 2 + core),
            ).start()
        remote(
            part(k, 0), part(k, 4), x_s.at[k], x_r.at[k], outer if QUARTERS[k] and k not in BOTH else inner
        ).start()

    def to_z(k, shards):
        for i, device in enumerate((below, above)):
            if QUARTERS[k]:
                spot = part(k, shards)
            else:
                spot = w_all.at[k, shards, run(half * 256 + i * 128, 128)]
            remote(spot, spot, z_s.at[k], z_r.at[k], device).start()

    def stage_x(k):
        drain(shape(k, 3, width(k)), y_r.at[k])
        moves = ((1, 1, inner), (2, 2, outer)) if k in BOTH else ((1, 3, outer),)
        for first, count, device in moves:
            remote(
                part(k, pl.ds(first, count)), part(k, pl.ds(4 + first, count)),
                x_s.at[k], x_r.at[k], device,
            ).start()
        to_z(k, pl.ds(1, 3))

    def stage_z(k):
        drain(shape(k, 4, width(k)), x_r.at[k])
        to_z(k, pl.ds(4, 4))

    def stage_f(k):
        if QUARTERS[k]:
            drain(shape(k, 7, 256), z_r.at[k])
            spot = w_all.at[k, pl.ds(1, 7), run(lax.rem(z + 3, 4) * 128, 64)]
            remote(spot, spot, f_s.at[k], f_r.at[k], above).start()
            spot = w_all.at[k, pl.ds(1, 7), run(lax.rem(z + 1, 4) * 128 + 64, 64)]
            remote(spot, spot, f_s.at[k], f_r.at[k], below).start()

    def arrived(k):
        if QUARTERS[k]:
            drain(shape(k, 7, 128), f_r.at[k])
        else:
            drain(shape(k, 7, 256), z_r.at[k])

    def at_step(i, late, stage):
        for k in range(max(late, 0), CHUNKS):
            pl.when(i == k - late)(lambda k=k: stage(k))

    def project(k):
        at_step(k, 0, arrived)

        def rows(m, _):
            at = pl.ds(pl.multiple_of(m * 512, 512), 512)
            qkv[at, :] = jnp.dot(
                x_all[at, :], w_all[k].reshape(CHIPS * 512, WIDE), preferred_element_type=F32
            ).astype(BF16)
            return 0

        lax.fori_loop(0, 2, rows, 0)

        def send(r, _):
            j = peer(r)
            snd[k, j] = jnp.dot(
                pack[pl.ds(pl.multiple_of(j * SLOTS, SLOTS), SLOTS), :], qkv[...],
                preferred_element_type=F32,
            ).astype(BF16)
            remote(
                snd.at[k, j], rcv.at[k, chip], a_s.at[k], a_r.at[k], (dp, j * 2 + core)
            ).start()
            return 0

        lax.fori_loop(1, CHIPS, send, 0)
        rcv[k, chip] = jnp.dot(
            pack[pl.ds(pl.multiple_of(chip * SLOTS, SLOTS), SLOTS), :], qkv[...],
            preferred_element_type=F32,
        ).astype(BF16)

    def placed(k, t):
        got = rcv[k, :, pl.ds(pl.multiple_of(t * 128, 128), 128), :].reshape(CHIPS * 128, WIDE)
        return jnp.dot(unpack[t], got, preferred_element_type=F32)

    def turned(v, t):
        at = pl.ds(pl.multiple_of(t * BLOCK, BLOCK), BLOCK)
        return (v * cos[at, :] + pltpu.roll(v, 64, 1) * sin[at, :]).astype(BF16)

    following = (dp, peer(1) * 2 + core)

    def halo(ref, i):
        remote(
            ref.at[:, pl.ds(1024, 512)], ref.at[:, pl.ds(0, 512)], h_s.at[i], h_r.at[i], following
        ).start()

    def receive(k):
        drain(rcv.at[k, pl.ds(0, 7)], a_r.at[k])

        def block(t, _):
            v = placed(k, t)
            for h in range(2):
                head = v[:, h * HEAD : (h + 1) * HEAD]

                @pl.when(k == 0)
                def _():
                    keys[h, pl.ds(pl.multiple_of(512 + t * 512, 512), 512), :] = turned(head, t)

                @pl.when(k == 1)
                def _():
                    vals[h, pl.ds(pl.multiple_of(512 + t * 512, 512), 512), :] = head.astype(BF16)

                @pl.when(k >= 2)
                def _():
                    qs[h, pl.ds(pl.multiple_of(t * 512, 512), 512), :] = turned(head, t)

            return 0

        lax.fori_loop(0, 2, block, 0)

        @pl.when(k == 0)
        def _():
            halo(keys, 0)

        @pl.when(k == 1)
        def _():
            halo(vals, 1)

        @pl.when(k == 2)
        def _():
            drain(keys.at[:, pl.ds(0, 512)], h_r.at[0])
            drain(vals.at[:, pl.ds(0, 512)], h_r.at[1])

        @pl.when(k >= 2)
        def _():
            attend(k - 2)

    def attend(c):
        g = c // 2

        def tile(n, _):
            i = lax.rem(n + other * 4, 8)
            at = pl.multiple_of(i * 128, 128)
            q = qs[:, pl.ds(at, 128), :].reshape(256, HEAD)
            s = lax.dot_general(
                q, keys[g, pl.ds(at, WINDOW), :], (((1,), (1,)), ((), ())),
                preferred_element_type=F32,
            )
            s = s.reshape(2, 128, WINDOW) * SCORE + bias[i][None]
            s = s.reshape(256, WINDOW)
            e = jnp.exp2(s - jnp.max(s, axis=1, keepdims=True))
            total = jnp.sum(e, axis=1, keepdims=True)
            o = jnp.dot(e.astype(BF16), vals[g, pl.ds(at, WINDOW), :], preferred_element_type=F32)
            o = (o / total).astype(BF16)
            to = pl.ds(pl.multiple_of(lax.rem(i, 4) * 128, 128), 128)
            outs[i // 4, c, to, pl.ds(0, HEAD)] = o[:128]
            outs[i // 4, c, to, pl.ds(HEAD, HEAD)] = o[128:]
            return 0

        lax.fori_loop(0, 4, tile, 0, unroll=4)
        spot = out.at[:, pl.ds(pl.multiple_of(core * 1024 + c * WIDE, WIDE), WIDE)]
        remote(outs.at[other, c], spot, o_s.at[c], o_r.at[c], sibling).start()
        lax.fori_loop(4, 8, tile, 0, unroll=4)
        pltpu.make_async_copy(outs.at[core, c], spot, o_l.at[c]).start()

    stage_y(0)
    for k in range(1, CHUNKS):
        shard_in(k)
    stage_y(1)
    stage_y(2)
    stage_y(3)
    drain(dests.at[core], dst_r)
    tri = (
        lax.broadcasted_iota(jnp.int32, (BLOCK, BLOCK), 0)
        <= lax.broadcasted_iota(jnp.int32, (BLOCK, BLOCK), 1)
    ).astype(BF16)
    targets = jnp.zeros((8, CHIPS * SLOTS), F32)
    for b in range(2):
        d = dests[b][:1]
        owner = lax.shift_right_logical(d, 9)
        hits = lax.broadcasted_iota(jnp.int32, (16, BLOCK), 0) == owner
        counts = jnp.dot(hits.astype(BF16), tri, preferred_element_type=F32)
        rank = jnp.sum(jnp.where(hits, counts, 0.0), axis=0, keepdims=True) - 1.0
        slot = (owner * 2 + b) * 64 + rank.astype(jnp.int32)

        def fill(m, _):
            at = pl.multiple_of(m * 256, 256)
            pack[pl.ds(at, 256), pl.ds(b * BLOCK, BLOCK)] = (
                lax.broadcasted_iota(jnp.int32, (256, BLOCK), 0) + at == slot
            ).astype(BF16)
            return 0

        lax.fori_loop(0, 8, fill, 0)
        target = jnp.bitwise_and(d, 511) + 1
        row = lax.broadcasted_iota(jnp.int32, (8, BLOCK), 0)
        digits = jnp.where(
            row == 0,
            lax.shift_right_logical(target, 5),
            jnp.where(row == 1, jnp.bitwise_and(target, 31), 0),
        )
        targets = targets + lax.dot_general(
            digits.astype(F32).astype(BF16), pack[:, b * BLOCK : (b + 1) * BLOCK],
            (((1,), (1,)), ((), ())), preferred_element_type=F32,
        )
    targets = targets[:1] * 32.0 + targets[1:2]
    for j in range(CHIPS):
        for t in range(2):
            at = (j * 2 + t) * 128
            meta_s[j, t : t + 1, :] = targets[:, at : at + 128]
        meta_s[j, 2:8, :] = jnp.zeros((6, 128), F32)
    for r in range(1, CHIPS):
        j = peer(r)
        remote(meta_s.at[j], meta_r.at[chip], met_s, met_r, (dp, j * 2 + core)).start()
    meta_r[chip] = meta_s[chip]

    stage_x(0)
    stage_y(4)

    for r in range(CHIPS):
        shard = (xl if r < 4 else 1 - xl) * 4 + at_y(r % 4)
        src = hid.at[:, run(shard * 512, 512)]
        spot = x_all.at[my_rows, pl.ds(r * 512, 512)]
        remote(src, spot, hid_s, hid_r, sibling).start()
        pltpu.make_async_copy(src, spot, hid_l).start()

    def mask(i, _):
        def doc(at):
            line = docs[pl.ds(jnp.maximum(at, 0), 1), :].astype(F32)
            return jnp.where(at >= 0, line, -1.0)

        own = jnp.transpose(jnp.broadcast_to(doc(chip * 8 + i), (128, 128)))
        row = lax.broadcasted_iota(jnp.int32, (128, 128), 0)
        for j in range(5):
            col = lax.broadcasted_iota(jnp.int32, (128, 128), 1) + j * 128
            seen = (col > row) & (col <= row + 512) & (own == doc(chip * 8 - 4 + i + j))
            bias[i, :, j * 128 : (j + 1) * 128] = jnp.where(seen, 0.0, -1e30)
        return 0

    lax.fori_loop(0, 8, mask, 0)

    stage_x(1)
    stage_y(5)
    stage_z(0)

    cc, cs = table[pl.ds(chip, 1), :], table[pl.ds(8 + chip, 1), :]
    turn[0] = table[16:48, :] * cc - table[48:80, :] * cs
    turn[1] = table[48:80, :] * cc + table[16:48, :] * cs
    sign = jnp.where(lax.broadcasted_iota(jnp.int32, (1, HEAD), 1) < 64, -1.0, 1.0)

    def rotary(i, _):
        at = run(i * 32, 32)
        ca, sa = turn[0, pl.ds(i, 1), :], turn[1, pl.ds(i, 1), :]
        cos[at, :] = table[80:112, :] * ca - table[112:144, :] * sa
        sin[at, :] = (table[112:144, :] * ca + table[80:112, :] * sa) * sign
        return 0

    lax.fori_loop(0, 32, rotary, 0)

    stage_x(2)
    stage_z(1)

    drain(meta_r.at[pl.ds(0, 7)], met_r)
    place = lax.broadcasted_iota(jnp.int32, (BLOCK, 128), 0).astype(F32) + 1.0
    for t in range(2):
        for i in range(CHIPS):
            unpack[t, :, i * 128 : (i + 1) * 128] = (place == meta_r[i, t : t + 1, :]).astype(BF16)

    drain(x_all.at[my_rows], hid_l)
    drain(x_all.at[my_rows], hid_r)

    def step(i, _):
        @pl.when(i < CHUNKS)
        def _():
            project(i)

        at_step(i, 1, stage_f)
        at_step(i, 2, stage_z)
        at_step(i, 3, stage_x)

        @pl.when(i >= 1)
        def _():
            receive(i - 1)

        return 0

    lax.fori_loop(0, CHUNKS + 1, step, 0)

    for c in range(4):
        spot = out.at[:, pl.ds(c * WIDE, WIDE)]
        drain(spot, o_l.at[c])
        drain(spot, o_r.at[c])
        drain(outs.at[0, c], o_s.at[c])
    for k in range(CHUNKS):
        drain(shape(k, 1, 256), w_s.at[k])
        drain(shape(k, 3, width(k)), y_s.at[k])
        drain(shape(k, 4, width(k)), x_s.at[k])
        drain(shape(k, 7, 256), z_s.at[k])
        if QUARTERS[k]:
            drain(shape(k, 7, 128), f_s.at[k])
        drain(snd.at[k, pl.ds(0, 7)], a_s.at[k])
    drain(keys.at[:, pl.ds(0, 512)], h_s.at[0])
    drain(vals.at[:, pl.ds(0, 512)], h_s.at[1])
    drain(x_all.at[my_rows], hid_s)
    drain(dests.at[core], dst_s)
    drain(meta_s.at[pl.ds(0, 7)], met_s)


def on_device(hidden, dest, doc_ids, w_query, key_weight, value_weight):
    anywhere = pl.BlockSpec(memory_space=pl.ANY)
    local = pl.BlockSpec(memory_space=pltpu.VMEM)
    return pl.pallas_call(
        kernel,
        out_shape=pltpu.VMEM((BLOCK, 2048), BF16),
        in_specs=[anywhere, local, local, local, anywhere, anywhere, anywhere],
        out_specs=local,
        scratch_shapes=[
            pltpu.VMEM((1024, HEAD), F32),
            pltpu.VMEM((1024, HEAD), F32),
            pltpu.VMEM((2, 32, HEAD), F32),
            pltpu.VMEM((1024, 4096), BF16),
            pltpu.VMEM((CHUNKS, CHIPS, 512, WIDE), BF16),
            pltpu.VMEM((2, 8, BLOCK), jnp.int32),
            pltpu.VMEM((CHIPS * SLOTS, 1024), BF16),
            pltpu.VMEM((2, BLOCK, 1024), BF16),
            pltpu.VMEM((CHIPS, 8, 128), F32),
            pltpu.VMEM((CHIPS, 8, 128), F32),
            pltpu.VMEM((1024, WIDE), BF16),
            pltpu.VMEM((CHUNKS, CHIPS, SLOTS, WIDE), BF16),
            pltpu.VMEM((CHUNKS, CHIPS, SLOTS, WIDE), BF16),
            pltpu.VMEM((2, 1536, HEAD), BF16),
            pltpu.VMEM((2, 1536, HEAD), BF16),
            pltpu.VMEM((2, 1024, HEAD), BF16),
            pltpu.VMEM((2, 4, BLOCK, WIDE), BF16),
            pltpu.VMEM((8, 128, WINDOW), F32),
            pltpu.SemaphoreType.DMA((7,)),
            pltpu.SemaphoreType.DMA((18, CHUNKS)),
        ],
        compiler_params=pltpu.CompilerParams(
            collective_id=0, has_side_effects=True, vmem_limit_bytes=60 * 2**20
        ),
    )(
        hidden, dest.reshape(1, BLOCK), doc_ids.reshape(64, 128), jnp.asarray(angles()),
        w_query, key_weight, value_weight,
    )


def solution(mesh):
    placed = (
        P(("dp", "ctx"), None),
        P(("dp", "ctx")),
        P("dp"),
        P("ctx", None),
        P("ctx", None),
        P("ctx", None),
    )
    return jax.shard_map(
        on_device, mesh=mesh, in_specs=placed, out_specs=P(("dp", "ctx"), None), check_vma=False
    )
```

```python
import jax
import jax.numpy as jnp
import numpy as np
from jax import lax
from jax.experimental import pallas as pl
from jax.experimental.pallas import tpu as pltpu
from jax.sharding import PartitionSpec as P

HEAD = 128
BLOCK = 512
CHIPS = 8
CHUNKS = 6
WIDE = 256
SLOTS = 256
WINDOW = 640
MESH = pl.DeviceIdType.MESH
rope_base = 500000.0 * 16.0 ** (128.0 / 126.0)
SCORE = HEAD**-0.5 * 1.4426950408889634
F32, BF16 = jnp.float32, jnp.bfloat16
QUARTERS = (False, False, False, False, True, True)


def angles():
    inverse = rope_base ** (-2.0 * np.arange(64) / HEAD)
    steps = [np.arange(8) * 1024, np.arange(32) * 32, np.arange(32)]
    parts = []
    for at in steps:
        angle = at[:, None] * inverse[None, :]
        parts += [np.tile(np.cos(angle), (1, 2)), np.tile(np.sin(angle), (1, 2))]
    return np.concatenate(parts).astype(np.float32)


def kernel(
    hid, dest, docs, table, wq, wk, wv, out,
    cos, sin, turn, x_all, w_all, dests, pack, unpack, meta_s, meta_r, qkv, snd, rcv, keys, vals, qs, outs, bias,
    one, six,
):
    dp, cx = lax.axis_index("dp"), lax.axis_index("ctx")
    z, xh = dp // 2, lax.rem(dp, 2)
    xl, y, core = cx // 8, lax.rem(cx // 2, 4), lax.rem(cx, 2)
    chip, half = cx // 2, lax.rem(z, 2)
    other = 1 - core

    def at_y(step):
        return lax.rem(y + step, 4)

    sibling = (dp, chip * 2 + other)
    inner = (dp, (1 - xl) * 8 + y * 2 + core)
    outer = (z * 2 + 1 - xh, (1 - xl) * 8 + y * 2 + core)
    above = (lax.rem(z + 1, 4) * 2 + xh, cx)
    below = (lax.rem(z + 3, 4) * 2 + xh, cx)

    def peer(step):
        return lax.rem(chip + step, CHIPS)

    (hid_l, hid_s, hid_r, dst_s, dst_r, met_s, met_r) = (one.at[i] for i in range(7))
    (w_l, w_s, w_r, y_s, y_r, x_s, x_r, z_s, z_r, a_s, a_r, h_s, h_r, o_l, o_s, o_r, f_s, f_r) = (
        six.at[i] for i in range(18)
    )

    barrier = pltpu.get_barrier_semaphore()
    near = [sibling, outer, above, below] + [(dp, peer(r) * 2 + core) for r in range(1, CHIPS)]
    for device in near:
        pl.semaphore_signal(barrier, inc=1, device_id=device, device_id_type=MESH)
    pl.semaphore_wait(barrier, len(near))

    def remote(src, dst, s, r, device):
        return pltpu.make_async_remote_copy(
            src_ref=src, dst_ref=dst, send_sem=s, recv_sem=r, device_id=device, device_id_type=MESH
        )

    def drain(ref, sem):
        pltpu.make_async_copy(ref, ref, sem).wait()

    def columns(k, of):
        if k == 0:
            return wk.at[:, pl.ds(pl.multiple_of(of * WIDE, WIDE), WIDE)]
        if k == 1:
            return wv.at[:, pl.ds(pl.multiple_of(of * WIDE, WIDE), WIDE)]
        return wq.at[:, pl.ds(pl.multiple_of(of * 1024 + (k - 2) * WIDE, WIDE), WIDE)]

    mine = pl.ds(pl.multiple_of(core * 256, 256), 256)
    my_rows = pl.ds(pl.multiple_of(core * BLOCK, BLOCK), BLOCK)
    def shard_in(k):
        spot = w_all.at[k, 0, mine]
        remote(columns(k, other), spot, w_s.at[k], w_r.at[k], sibling).start()
        pltpu.make_async_copy(columns(k, core), spot, w_l.at[k]).start()

    shard_in(0)
    dests[core] = jnp.broadcast_to(dest[...], (8, BLOCK))
    remote(dests.at[core], dests.at[core], dst_s, dst_r, sibling).start()

    def run(start, size):
        return pl.ds(pl.multiple_of(start, size), size)

    def part(k, shards):
        rows = run(z * 128, 128) if QUARTERS[k] else run(half * 256, 256)
        return w_all.at[k, shards, rows]

    def shape(k, n, rows):
        return w_all.at[k, pl.ds(0, n), pl.ds(0, rows)]

    def width(k):
        return 128 if QUARTERS[k] else 256

    def stage_y(k):
        own = w_all.at[k, 0, mine]
        drain(own, w_l.at[k])
        drain(own, w_r.at[k])
        for step in (1, 3, 2):
            remote(
                part(k, 0), part(k, 4 - step), y_s.at[k], y_r.at[k],
                (dp, xl * 8 + at_y(step) * 2 + core),
            ).start()
        remote(
            part(k, 0), part(k, 4), x_s.at[k], x_r.at[k], outer if QUARTERS[k] and k != 5 else inner
        ).start()

    def to_z(k, shards):
        for i, device in enumerate((below, above)):
            if QUARTERS[k]:
                spot = part(k, shards)
            else:
                spot = w_all.at[k, shards, run(half * 256 + i * 128, 128)]
            remote(spot, spot, z_s.at[k], z_r.at[k], device).start()

    def stage_x(k):
        drain(shape(k, 3, width(k)), y_r.at[k])
        moves = ((1, 1, inner), (2, 2, outer)) if k in (0, 5) else ((1, 3, outer),)
        for first, count, device in moves:
            remote(
                part(k, pl.ds(first, count)), part(k, pl.ds(4 + first, count)),
                x_s.at[k], x_r.at[k], device,
            ).start()
        to_z(k, pl.ds(1, 3))

    def stage_z(k):
        drain(shape(k, 4, width(k)), x_r.at[k])
        to_z(k, pl.ds(4, 4))

    def stage_f(k):
        if QUARTERS[k]:
            drain(shape(k, 7, 256), z_r.at[k])
            spot = w_all.at[k, pl.ds(1, 7), run(lax.rem(z + 3, 4) * 128, 64)]
            remote(spot, spot, f_s.at[k], f_r.at[k], above).start()
            spot = w_all.at[k, pl.ds(1, 7), run(lax.rem(z + 1, 4) * 128 + 64, 64)]
            remote(spot, spot, f_s.at[k], f_r.at[k], below).start()

    def arrived(k):
        if QUARTERS[k]:
            drain(shape(k, 7, 128), f_r.at[k])
        else:
            drain(shape(k, 7, 256), z_r.at[k])

    def at_step(i, late, stage):
        for k in range(max(late, 0), CHUNKS):
            pl.when(i == k - late)(lambda k=k: stage(k))

    def project(k):
        at_step(k, 0, arrived)

        def rows(m, _):
            at = pl.ds(pl.multiple_of(m * 512, 512), 512)
            qkv[at, :] = jnp.dot(
                x_all[at, :], w_all[k].reshape(CHIPS * 512, WIDE), preferred_element_type=F32
            ).astype(BF16)
            return 0

        lax.fori_loop(0, 2, rows, 0)

        def send(r, _):
            j = peer(r)
            snd[k, j] = jnp.dot(
                pack[pl.ds(pl.multiple_of(j * SLOTS, SLOTS), SLOTS), :], qkv[...],
                preferred_element_type=F32,
            ).astype(BF16)
            remote(
                snd.at[k, j], rcv.at[k, chip], a_s.at[k], a_r.at[k], (dp, j * 2 + core)
            ).start()
            return 0

        lax.fori_loop(1, CHIPS, send, 0)
        rcv[k, chip] = jnp.dot(
            pack[pl.ds(pl.multiple_of(chip * SLOTS, SLOTS), SLOTS), :], qkv[...],
            preferred_element_type=F32,
        ).astype(BF16)

    def placed(k, t):
        got = rcv[k, :, pl.ds(pl.multiple_of(t * 128, 128), 128), :].reshape(CHIPS * 128, WIDE)
        return jnp.dot(unpack[t], got, preferred_element_type=F32)

    def turned(v, t):
        at = pl.ds(pl.multiple_of(t * BLOCK, BLOCK), BLOCK)
        return (v * cos[at, :] + pltpu.roll(v, 64, 1) * sin[at, :]).astype(BF16)

    following = (dp, peer(1) * 2 + core)

    def halo(ref, i):
        remote(
            ref.at[:, pl.ds(1024, 512)], ref.at[:, pl.ds(0, 512)], h_s.at[i], h_r.at[i], following
        ).start()

    def receive(k):
        drain(rcv.at[k, pl.ds(0, 7)], a_r.at[k])

        def block(t, _):
            v = placed(k, t)
            for h in range(2):
                head = v[:, h * HEAD : (h + 1) * HEAD]

                @pl.when(k == 0)
                def _():
                    keys[h, pl.ds(pl.multiple_of(512 + t * 512, 512), 512), :] = turned(head, t)

                @pl.when(k == 1)
                def _():
                    vals[h, pl.ds(pl.multiple_of(512 + t * 512, 512), 512), :] = head.astype(BF16)

                @pl.when(k >= 2)
                def _():
                    qs[h, pl.ds(pl.multiple_of(t * 512, 512), 512), :] = turned(head, t)

            return 0

        lax.fori_loop(0, 2, block, 0)

        @pl.when(k == 0)
        def _():
            halo(keys, 0)

        @pl.when(k == 1)
        def _():
            halo(vals, 1)

        @pl.when(k == 2)
        def _():
            drain(keys.at[:, pl.ds(0, 512)], h_r.at[0])
            drain(vals.at[:, pl.ds(0, 512)], h_r.at[1])

        @pl.when(k >= 2)
        def _():
            attend(k - 2)

    def attend(c):
        g = c // 2

        def tile(n, _):
            i = lax.rem(n + other * 4, 8)
            at = pl.multiple_of(i * 128, 128)
            q = qs[:, pl.ds(at, 128), :].reshape(256, HEAD)
            s = lax.dot_general(
                q, keys[g, pl.ds(at, WINDOW), :], (((1,), (1,)), ((), ())),
                preferred_element_type=F32,
            )
            s = s.reshape(2, 128, WINDOW) * SCORE + bias[i][None]
            s = s.reshape(256, WINDOW)
            e = jnp.exp2(s - jnp.max(s, axis=1, keepdims=True))
            total = jnp.sum(e, axis=1, keepdims=True)
            o = jnp.dot(e.astype(BF16), vals[g, pl.ds(at, WINDOW), :], preferred_element_type=F32)
            o = (o / total).astype(BF16)
            to = pl.ds(pl.multiple_of(lax.rem(i, 4) * 128, 128), 128)
            outs[i // 4, c, to, pl.ds(0, HEAD)] = o[:128]
            outs[i // 4, c, to, pl.ds(HEAD, HEAD)] = o[128:]
            return 0

        lax.fori_loop(0, 4, tile, 0, unroll=4)
        spot = out.at[:, pl.ds(pl.multiple_of(core * 1024 + c * WIDE, WIDE), WIDE)]
        remote(outs.at[other, c], spot, o_s.at[c], o_r.at[c], sibling).start()
        lax.fori_loop(4, 8, tile, 0, unroll=4)
        pltpu.make_async_copy(outs.at[core, c], spot, o_l.at[c]).start()

    stage_y(0)
    for k in range(1, CHUNKS):
        shard_in(k)
    stage_y(1)
    stage_y(2)
    stage_y(3)
    drain(dests.at[core], dst_r)
    tri = (
        lax.broadcasted_iota(jnp.int32, (BLOCK, BLOCK), 0)
        <= lax.broadcasted_iota(jnp.int32, (BLOCK, BLOCK), 1)
    ).astype(BF16)
    targets = jnp.zeros((8, CHIPS * SLOTS), F32)
    for b in range(2):
        d = dests[b][:1]
        owner = lax.shift_right_logical(d, 9)
        hits = lax.broadcasted_iota(jnp.int32, (16, BLOCK), 0) == owner
        counts = jnp.dot(hits.astype(BF16), tri, preferred_element_type=F32)
        rank = jnp.sum(jnp.where(hits, counts, 0.0), axis=0, keepdims=True) - 1.0
        slot = (owner * 2 + b) * 64 + rank.astype(jnp.int32)

        def fill(m, _):
            at = pl.multiple_of(m * 256, 256)
            pack[pl.ds(at, 256), pl.ds(b * BLOCK, BLOCK)] = (
                lax.broadcasted_iota(jnp.int32, (256, BLOCK), 0) + at == slot
            ).astype(BF16)
            return 0

        lax.fori_loop(0, 8, fill, 0)
        target = jnp.bitwise_and(d, 511) + 1
        row = lax.broadcasted_iota(jnp.int32, (8, BLOCK), 0)
        digits = jnp.where(
            row == 0,
            lax.shift_right_logical(target, 5),
            jnp.where(row == 1, jnp.bitwise_and(target, 31), 0),
        )
        targets = targets + lax.dot_general(
            digits.astype(F32).astype(BF16), pack[:, b * BLOCK : (b + 1) * BLOCK],
            (((1,), (1,)), ((), ())), preferred_element_type=F32,
        )
    targets = targets[:1] * 32.0 + targets[1:2]
    for j in range(CHIPS):
        for t in range(2):
            at = (j * 2 + t) * 128
            meta_s[j, t : t + 1, :] = targets[:, at : at + 128]
        meta_s[j, 2:8, :] = jnp.zeros((6, 128), F32)
    for r in range(1, CHIPS):
        j = peer(r)
        remote(meta_s.at[j], meta_r.at[chip], met_s, met_r, (dp, j * 2 + core)).start()
    meta_r[chip] = meta_s[chip]

    stage_x(0)
    stage_y(4)

    for r in range(CHIPS):
        shard = (xl if r < 4 else 1 - xl) * 4 + at_y(r % 4)
        src = hid.at[:, run(shard * 512, 512)]
        spot = x_all.at[my_rows, pl.ds(r * 512, 512)]
        remote(src, spot, hid_s, hid_r, sibling).start()
        pltpu.make_async_copy(src, spot, hid_l).start()

    def mask(i, _):
        def doc(at):
            line = docs[pl.ds(jnp.maximum(at, 0), 1), :].astype(F32)
            return jnp.where(at >= 0, line, -1.0)

        own = jnp.transpose(jnp.broadcast_to(doc(chip * 8 + i), (128, 128)))
        row = lax.broadcasted_iota(jnp.int32, (128, 128), 0)
        for j in range(5):
            col = lax.broadcasted_iota(jnp.int32, (128, 128), 1) + j * 128
            seen = (col > row) & (col <= row + 512) & (own == doc(chip * 8 - 4 + i + j))
            bias[i, :, j * 128 : (j + 1) * 128] = jnp.where(seen, 0.0, -1e30)
        return 0

    lax.fori_loop(0, 8, mask, 0)

    stage_x(1)
    stage_y(5)
    stage_z(0)

    cc, cs = table[pl.ds(chip, 1), :], table[pl.ds(8 + chip, 1), :]
    turn[0] = table[16:48, :] * cc - table[48:80, :] * cs
    turn[1] = table[48:80, :] * cc + table[16:48, :] * cs
    sign = jnp.where(lax.broadcasted_iota(jnp.int32, (1, HEAD), 1) < 64, -1.0, 1.0)

    def rotary(i, _):
        at = run(i * 32, 32)
        ca, sa = turn[0, pl.ds(i, 1), :], turn[1, pl.ds(i, 1), :]
        cos[at, :] = table[80:112, :] * ca - table[112:144, :] * sa
        sin[at, :] = (table[112:144, :] * ca + table[80:112, :] * sa) * sign
        return 0

    lax.fori_loop(0, 32, rotary, 0)

    stage_x(2)
    stage_z(1)

    drain(meta_r.at[pl.ds(0, 7)], met_r)
    place = lax.broadcasted_iota(jnp.int32, (BLOCK, 128), 0).astype(F32) + 1.0
    for t in range(2):
        for i in range(CHIPS):
            unpack[t, :, i * 128 : (i + 1) * 128] = (place == meta_r[i, t : t + 1, :]).astype(BF16)

    drain(x_all.at[my_rows], hid_l)
    drain(x_all.at[my_rows], hid_r)

    def step(i, _):
        @pl.when(i < CHUNKS)
        def _():
            project(i)

        at_step(i, 3, stage_x)
        at_step(i, 2, stage_z)
        at_step(i, 1, stage_f)

        @pl.when(i >= 1)
        def _():
            receive(i - 1)

        return 0

    lax.fori_loop(0, CHUNKS + 1, step, 0)

    for c in range(4):
        spot = out.at[:, pl.ds(c * WIDE, WIDE)]
        drain(spot, o_l.at[c])
        drain(spot, o_r.at[c])
        drain(outs.at[0, c], o_s.at[c])
    for k in range(CHUNKS):
        drain(shape(k, 1, 256), w_s.at[k])
        drain(shape(k, 3, width(k)), y_s.at[k])
        drain(shape(k, 4, width(k)), x_s.at[k])
        drain(shape(k, 7, 256), z_s.at[k])
        if QUARTERS[k]:
            drain(shape(k, 7, 128), f_s.at[k])
        drain(snd.at[k, pl.ds(0, 7)], a_s.at[k])
    drain(keys.at[:, pl.ds(0, 512)], h_s.at[0])
    drain(vals.at[:, pl.ds(0, 512)], h_s.at[1])
    drain(x_all.at[my_rows], hid_s)
    drain(dests.at[core], dst_s)
    drain(meta_s.at[pl.ds(0, 7)], met_s)


def on_device(hidden, dest, doc_ids, w_query, key_weight, value_weight):
    anywhere = pl.BlockSpec(memory_space=pl.ANY)
    local = pl.BlockSpec(memory_space=pltpu.VMEM)
    return pl.pallas_call(
        kernel,
        out_shape=pltpu.VMEM((BLOCK, 2048), BF16),
        in_specs=[anywhere, local, local, local, anywhere, anywhere, anywhere],
        out_specs=local,
        scratch_shapes=[
            pltpu.VMEM((1024, HEAD), F32),
            pltpu.VMEM((1024, HEAD), F32),
            pltpu.VMEM((2, 32, HEAD), F32),
            pltpu.VMEM((1024, 4096), BF16),
            pltpu.VMEM((CHUNKS, CHIPS, 512, WIDE), BF16),
            pltpu.VMEM((2, 8, BLOCK), jnp.int32),
            pltpu.VMEM((CHIPS * SLOTS, 1024), BF16),
            pltpu.VMEM((2, BLOCK, 1024), BF16),
            pltpu.VMEM((CHIPS, 8, 128), F32),
            pltpu.VMEM((CHIPS, 8, 128), F32),
            pltpu.VMEM((1024, WIDE), BF16),
            pltpu.VMEM((CHUNKS, CHIPS, SLOTS, WIDE), BF16),
            pltpu.VMEM((CHUNKS, CHIPS, SLOTS, WIDE), BF16),
            pltpu.VMEM((2, 1536, HEAD), BF16),
            pltpu.VMEM((2, 1536, HEAD), BF16),
            pltpu.VMEM((2, 1024, HEAD), BF16),
            pltpu.VMEM((2, 4, BLOCK, WIDE), BF16),
            pltpu.VMEM((8, 128, WINDOW), F32),
            pltpu.SemaphoreType.DMA((7,)),
            pltpu.SemaphoreType.DMA((18, CHUNKS)),
        ],
        compiler_params=pltpu.CompilerParams(
            collective_id=0, has_side_effects=True, vmem_limit_bytes=60 * 2**20
        ),
    )(
        hidden, dest.reshape(1, BLOCK), doc_ids.reshape(64, 128), jnp.asarray(angles()),
        w_query, key_weight, value_weight,
    )


def solution(mesh):
    placed = (
        P(("dp", "ctx"), None),
        P(("dp", "ctx")),
        P("dp"),
        P("ctx", None),
        P("ctx", None),
        P("ctx", None),
    )
    return jax.shard_map(
        on_device, mesh=mesh, in_specs=placed, out_specs=P(("dp", "ctx"), None), check_vma=False
    )
```
